32 devices in a mesh: col: 8 (over y, x, core), sub: 4 (over z).
Axes of the slice: x: 2, y: 2, z: 4, core: 2. Of those that a mesh axis runs over, the one named last changes fastest.
Arguments:
- vectors: bfloat16 [131072, 128], P(('col', 'sub')), may hold values from -6 to 6
- near_blocks: bfloat16 [512, 4, 256, 256], P(('col', 'sub')), may hold values from -0.1875 to 0.1875
- near_index: int32 [512, 4], P(('col', 'sub')), may hold values from 0 to 511, as said below
- leaf_basis: bfloat16 [512, 32, 256], P(('col', 'sub')), may hold values from -0.375 to 0.375
- leaf_transfer: float32 [512, 32, 32], P(('col', 'sub')), may hold values from -0.25 to 0.25
- leaf_coupling: float32 [512, 8, 32, 32], P(('col', 'sub')), may hold values from -0.375 to 0.375
- leaf_far: int32 [512, 8], P(('col', 'sub')), may hold values from 0 to 511, as said below
- cluster_transfer: float32 [32, 32, 32], P(('col', 'sub')), may hold values from -0.5 to 0.5
- cluster_coupling: float32 [32, 4, 32, 32], P(('col', 'sub')), may hold values from -0.5 to 0.5
- cluster_partner: int32 [32, 4], P(('col', 'sub')), may hold values from 0 to 3
- top_coupling: float32 [8, 8, 32, 32], P('col'), may hold values from -0.375 to 0.375
- top_partner: int32 [8, 8], P('col'), may hold values from 0 to 7
Outputs:
- products: bfloat16 [131072, 128], P(('col', 'sub'))
The draws below stay inside these ranges and needn't reach their ends.
Inputs may be any that keep to these rules, and one draw needn't show every extreme that they name: `near_index`: slot 0 of leaf i is i itself; every entry lies within 16 leaves of i; slot 1 is exactly 16 leaves away from i. `leaf_far`: every entry lies within 16 leaves of its row leaf i; slots 0 and 1 are exactly 16 leaves away from i.
All inputs are finite; a program needn't handle non-finite values.
Results may differ from the reference program's by a relative error of at most 0.0034.
Values may be sent and summed in bfloat16 or wider, within the bound.
No kernel may reach another device: no remote copies, remote signals or barrier semaphores. Data moves between devices by JAX's collectives and lax.ppermute only.
A program may use at most 64 MiB of HBM per device.

```python
import jax
import jax.numpy as jnp
from jax import lax

LEAF = 256
RANK = 32
LD = 16
NEAR = 4
FAR0 = 8
FAR1 = 4
FAR2 = 8
COLS = 128
LEAVES = 512
NPTS = 131072
N_COL = 8
N_SUB = 4


def draw_near_index(key, part):
    leaf_ids = jnp.arange(LEAVES, dtype=jnp.int32)
    stride = jnp.where(leaf_ids + LD < LEAVES, LD, -LD).astype(jnp.int32)
    offsets = jax.random.randint(jax.random.fold_in(key, 11), (LEAVES, NEAR - 2), -LD, LD + 1, dtype=jnp.int32)
    others = jnp.clip(leaf_ids[:, None] + offsets, 0, LEAVES - 1)
    return jnp.concatenate([leaf_ids[:, None], (leaf_ids + stride)[:, None], others], axis=1).astype(jnp.int32)


def draw_leaf_far(key, part):
    leaf_ids = jnp.arange(LEAVES, dtype=jnp.int32)
    first_slot = jnp.where(leaf_ids >= LD, leaf_ids - LD, leaf_ids + LD).astype(jnp.int32)
    second_slot = jnp.where(leaf_ids + LD < LEAVES, leaf_ids + LD, leaf_ids - LD).astype(jnp.int32)
    offsets = jax.random.randint(jax.random.fold_in(key, 23), (LEAVES, FAR0 - 2), -LD, LD + 1, dtype=jnp.int32)
    others = jnp.clip(leaf_ids[:, None] + offsets, 0, LEAVES - 1)
    return jnp.concatenate([first_slot[:, None], second_slot[:, None], others], axis=1).astype(jnp.int32)


def place_ends(array, key, least, high):
    longest = array.shape.index(max(array.shape))
    spots = []
    for shift in (0, 1):
        where = [jax.random.randint(jax.random.fold_in(key, axis), (), 0, length) for axis, length in enumerate(array.shape)]
        where[longest] = (where[longest] + shift) % array.shape[longest]
        spots.append(tuple(where))
    return array.at[spots[0]].set(least).at[spots[1]].set(high)


def levels(key, dims, split, low, largest):
    loudness, own = 1.0, jax.random.fold_in(key, 6)
    for axis_at, shards_of in split:
        heights = jnp.exp(jax.random.uniform(jax.random.fold_in(own, axis_at), (shards_of,), jnp.float32, low / len(split), largest / len(split)))
        loudness = loudness * jnp.repeat(heights, dims[axis_at] // shards_of).reshape([-1 if axis == axis_at else 1 for axis in range(len(dims))])
    return loudness


def scatter_about(key, dims, width, limit, cuts=(), kind=jnp.bfloat16):
    factor_of = levels(key, dims, cuts, -0.22, 0.18) if cuts else 1.0
    drawn = jax.random.normal(key, dims, jnp.float32) * width * factor_of
    return jnp.minimum(jnp.maximum(drawn, -limit), limit).astype(kind)


def setup_inputs(seed: int = 0) -> dict:
    splits = jax.random.split(jax.random.key(seed), 13)
    return {
        "vectors": scatter_about(splits[0], (NPTS, COLS), 1.0, 6.0, ((0, 32),)),
        "near_blocks": scatter_about(splits[1], (LEAVES, NEAR, LEAF, LEAF), (LEAF * NEAR) ** -0.5, 0.1875, ((0, 32),)),
        "near_index": draw_near_index(jax.random.fold_in(splits[12], 71), 0),
        "leaf_basis": scatter_about(splits[3], (LEAVES, RANK, LEAF), LEAF ** -0.5, 0.375, ((0, 32),)),
        "leaf_transfer": scatter_about(splits[4], (LEAVES, RANK, RANK), (RANK * LD) ** -0.5, 0.25, ((0, 32),), jnp.float32),
        "leaf_coupling": scatter_about(splits[5], (LEAVES, FAR0, RANK, RANK), (RANK * FAR0) ** -0.5, 0.375, ((0, 32),), jnp.float32),
        "leaf_far": draw_leaf_far(jax.random.fold_in(splits[12], 71), 0),
        "cluster_transfer": scatter_about(splits[7], (N_COL * N_SUB, RANK, RANK), (RANK * N_SUB) ** -0.5, 0.5, ((0, 32),), jnp.float32),
        "cluster_coupling": scatter_about(splits[8], (N_COL * N_SUB, FAR1, RANK, RANK), (RANK * FAR1) ** -0.5, 0.5, ((0, 32),), jnp.float32),
        "cluster_partner": place_ends(jax.random.randint(splits[9], (N_COL * N_SUB, FAR1), 0, N_SUB), jax.random.fold_in(splits[9], 1), 0, N_SUB - 1).astype(jnp.int32),
        "top_coupling": scatter_about(splits[10], (N_COL, FAR2, RANK, RANK), (RANK * FAR2) ** -0.5, 0.375, ((0, 8),), jnp.float32),
        "top_partner": place_ends(jax.random.randint(splits[11], (N_COL, FAR2), 0, N_COL), jax.random.fold_in(splits[11], 1), 0, N_COL - 1).astype(jnp.int32),
    }


HIGHEST = lax.Precision.HIGHEST


def reference(vectors, near_blocks, near_index, leaf_basis, leaf_transfer, leaf_coupling, leaf_far, cluster_transfer, cluster_coupling, cluster_partner, top_coupling, top_partner):
    group_count = N_COL * N_SUB
    leaf_count = group_count * LD
    leaf_vec = vectors.reshape(leaf_count, LEAF, COLS)

    def basis_apply(pieces):
        basis, local_vec = pieces
        return jnp.einsum('lrp,lpc->lrc', basis.astype(jnp.float32), local_vec.astype(jnp.float32), precision=HIGHEST)

    leaf_coefs = lax.map(basis_apply, (leaf_basis.reshape(group_count, LD, RANK, LEAF), leaf_vec.reshape(group_count, LD, LEAF, COLS))).reshape(leaf_count, RANK, COLS)
    cluster_coefs = jnp.einsum('lrs,lrc->lsc', leaf_transfer, leaf_coefs, precision=HIGHEST).reshape(group_count, LD, RANK, COLS).sum(axis=1)
    upward = jnp.einsum('drs,drc->dsc', cluster_transfer, cluster_coefs, precision=HIGHEST)
    top_coefs = upward.reshape(N_COL, N_SUB, RANK, COLS).sum(axis=1)
    top_field = jnp.einsum('qkrs,qksc->qrc', top_coupling, top_coefs[top_partner], precision=HIGHEST)
    group_base = (jnp.arange(group_count, dtype=jnp.int32) // N_SUB) * N_SUB
    partner_global = (group_base[:, None] + cluster_partner).astype(jnp.int32)
    cluster_field = jnp.einsum('dkrs,dksc->drc', cluster_coupling, cluster_coefs[partner_global], precision=HIGHEST)
    cluster_field = cluster_field + jnp.einsum('drs,dsc->drc', cluster_transfer, jnp.repeat(top_field, N_SUB, axis=0), precision=HIGHEST)

    def group_output(pieces):
        blocks, near_here, far_here, coupling, transfer, basis, parent = pieces
        leaf_field = jnp.einsum('lkrs,lksc->lrc', coupling, leaf_coefs[far_here], precision=HIGHEST)
        leaf_field = leaf_field + jnp.einsum('lrs,sc->lrc', transfer, parent, precision=HIGHEST)
        rounded = lax.optimization_barrier(leaf_field.astype(jnp.bfloat16)).astype(jnp.float32)
        picked = leaf_vec[near_here].astype(jnp.float32)
        near_part = jnp.einsum('lkij,lkjc->lic', blocks.astype(jnp.float32), picked, precision=HIGHEST)
        far_part = jnp.einsum('lrp,lrc->lpc', basis.astype(jnp.float32), rounded, precision=HIGHEST)
        return (near_part + far_part).astype(jnp.bfloat16)

    result = lax.map(group_output, (
        near_blocks.reshape(group_count, LD, NEAR, LEAF, LEAF),
        near_index.reshape(group_count, LD, NEAR),
        leaf_far.reshape(group_count, LD, FAR0),
        leaf_coupling.reshape(group_count, LD, FAR0, RANK, RANK),
        leaf_transfer.reshape(group_count, LD, RANK, RANK),
        leaf_basis.reshape(group_count, LD, RANK, LEAF),
        cluster_field))
    return result.reshape(leaf_count * LEAF, COLS)
```

```python
import functools

import jax
import jax.numpy as jnp
from jax import lax
from jax.experimental import pallas as pl
from jax.experimental.pallas import tpu as pltpu
from jax.sharding import PartitionSpec as P

HIGHEST = lax.Precision.HIGHEST
BOTH = ("col", "sub")


def shift(value, step):
    count = lax.axis_size(BOTH)
    pairs = [(i, i + step) for i in range(count) if 0 <= i + step < count]
    return lax.ppermute(value, BOTH, pairs)


def gather_sub(value):
    count = lax.axis_size("sub")
    parts = [value]
    for step in range(1, count):
        pairs = [(i, (i + step) % count) for i in range(count)]
        parts.append(lax.ppermute(value, "sub", pairs))
    return jnp.stack(parts)


def gather_col(value):
    count = lax.axis_size("col")
    if count & (count - 1):
        return lax.all_gather(value, "col", axis=0), jnp.arange(count)
    stack = value[None]
    width = 1
    while width < count:
        pairs = [(i, i ^ width) for i in range(count)]
        stack = jnp.concatenate([stack, lax.ppermute(stack, "col", pairs)], axis=0)
        width *= 2
    return stack, jnp.arange(count) ^ lax.axis_index("col")


def near_first_body(leaves, slots, place_ref, blocks_ref, own_ref, high_ref, acc_ref):
    leaf = pl.program_id(0)
    rows = acc_ref.shape[0]
    acc_ref[...] = jnp.zeros_like(acc_ref)
    for k in range(slots):
        place = place_ref[leaf, k]

        def add(vec_ref, at, k=k):
            start = pl.multiple_of(at * rows, rows)
            acc_ref[...] += jnp.dot(
                blocks_ref[0, k], vec_ref[pl.ds(start, rows), :], preferred_element_type=jnp.float32
            )

        pl.when((place >= leaves) & (place < 2 * leaves))(lambda: add(own_ref, place - leaves))
        pl.when(place >= 2 * leaves)(lambda: add(high_ref, place - 2 * leaves))


def near_first(place, blocks, own, high):
    leaves, slots, rows, _ = blocks.shape
    columns = own.shape[1]
    whole = pl.BlockSpec((leaves * rows, columns), lambda i, p: (0, 0))
    return pl.pallas_call(
        functools.partial(near_first_body, leaves, slots),
        grid_spec=pltpu.PrefetchScalarGridSpec(
            num_scalar_prefetch=1,
            grid=(leaves,),
            in_specs=[
                pl.BlockSpec((1, slots, rows, rows), lambda i, p: (i, 0, 0, 0)),
                whole,
                whole,
            ],
            out_specs=pl.BlockSpec((rows, columns), lambda i, p: (i, 0)),
        ),
        out_shape=jax.ShapeDtypeStruct((leaves * rows, columns), jnp.float32),
        compiler_params=pltpu.CompilerParams(vmem_limit_bytes=24 * 2**20),
        cost_estimate=pl.CostEstimate(
            flops=2 * leaves * slots * rows * rows * columns,
            bytes_accessed=2 * leaves * slots * rows * rows,
            transcendentals=0,
        ),
        name="near_own_high",
    )(place, blocks, own, high)


def near_last_body(leaves, slots, place_ref, blocks_ref, low_ref, acc_ref, out_ref, held, sems):
    rows = held.shape[1]

    def copy(at):
        return pltpu.make_async_copy(
            blocks_ref.at[at // slots, lax.rem(at, slots)], held.at[at], sems.at[at]
        )

    @pl.loop(0, leaves * slots)
    def _(at):
        @pl.when(place_ref[at] < leaves)
        def _():
            copy(at).start()

    @pl.loop(0, leaves)
    def _(leaf):
        here = pl.ds(pl.multiple_of(leaf * rows, rows), rows)
        for k in range(slots):
            at = leaf * slots + k
            place = place_ref[at]

            @pl.when(place < leaves)
            def _():
                copy(at).wait()
                start = pl.multiple_of(place * rows, rows)
                acc_ref[here, :] += jnp.dot(
                    held[at], low_ref[pl.ds(start, rows), :], preferred_element_type=jnp.float32
                )

        out_ref[here, :] = acc_ref[here, :].astype(out_ref.dtype)


def near_last(place, blocks, low, acc):
    leaves, slots, rows, _ = blocks.shape
    columns = low.shape[1]
    return pl.pallas_call(
        functools.partial(near_last_body, leaves, slots),
        in_specs=[
            pl.BlockSpec(memory_space=pltpu.SMEM),
            pl.BlockSpec(memory_space=pl.ANY),
            pl.BlockSpec(memory_space=pltpu.VMEM),
            pl.BlockSpec(memory_space=pltpu.VMEM),
        ],
        out_specs=pl.BlockSpec(memory_space=pltpu.VMEM),
        out_shape=jax.ShapeDtypeStruct((leaves * rows, columns), low.dtype),
        scratch_shapes=[
            pltpu.VMEM((leaves * slots, rows, rows), blocks.dtype),
            pltpu.SemaphoreType.DMA((leaves * slots,)),
        ],
        compiler_params=pltpu.CompilerParams(vmem_limit_bytes=24 * 2**20),
        cost_estimate=pl.CostEstimate(
            flops=leaves * rows * rows * columns, bytes_accessed=4 * 2**20, transcendentals=0
        ),
        name="near_low",
    )(place.reshape(-1), blocks, low, acc)


def local(
    vectors,
    near_blocks,
    near_index,
    leaf_basis,
    leaf_transfer,
    leaf_coupling,
    leaf_far,
    cluster_transfer,
    cluster_coupling,
    cluster_partner,
    top_coupling,
    top_partner,
):
    leaves, rank, rows = leaf_basis.shape
    columns = vectors.shape[1]
    sub = lax.axis_index("sub")
    subs = lax.axis_size("sub")
    window_start = lax.axis_index(BOTH) * leaves - leaves

    high_vec = shift(vectors, -1)

    own_vec = vectors.reshape(leaves, rows, columns)
    leaf_coefs = jnp.einsum("lrp,lpc->lrc", leaf_basis, own_vec, preferred_element_type=jnp.float32)
    cluster_coef = jnp.einsum("lrs,lrc->sc", leaf_transfer, leaf_coefs, precision=HIGHEST)
    upward = jnp.dot(cluster_transfer[0].T, cluster_coef, precision=HIGHEST)
    gathered = gather_sub(jnp.stack([cluster_coef, upward]))

    low_coefs = shift(leaf_coefs, 1)
    high_coefs = shift(leaf_coefs, -1)
    later_vec, _ = lax.optimization_barrier((vectors, upward))
    low_vec = shift(later_vec, 1)

    col_coefs, col_place = gather_col(gathered[:, 1].sum(axis=0))
    sub_place = lax.rem(sub - cluster_partner[0] + subs, subs)
    cluster_field = jnp.einsum(
        "krs,ksc->rc", cluster_coupling[0], gathered[sub_place, 0], precision=HIGHEST
    )
    top_field = jnp.einsum(
        "krs,ksc->rc", top_coupling[0], col_coefs[col_place[top_partner[0]]], precision=HIGHEST
    )
    cluster_field = cluster_field + jnp.dot(cluster_transfer[0], top_field, precision=HIGHEST)

    near_place = jnp.clip(near_index - window_start, 0, 3 * leaves - 1)
    acc = near_first(near_place, near_blocks, vectors, high_vec)

    window_coefs = jnp.concatenate([low_coefs, leaf_coefs, high_coefs], axis=0)
    far_coefs = window_coefs[leaf_far - window_start]
    leaf_field = jnp.einsum("lkrs,lksc->lrc", leaf_coupling, far_coefs, precision=HIGHEST)
    leaf_field = leaf_field + jnp.einsum(
        "lrs,sc->lrc", leaf_transfer, cluster_field, precision=HIGHEST
    )
    rounded = leaf_field.astype(jnp.bfloat16)
    far_part = jnp.einsum("lrp,lrc->lpc", leaf_basis, rounded, preferred_element_type=jnp.float32)
    acc = acc + far_part.reshape(leaves * rows, columns)
    return near_last(near_place, near_blocks, low_vec, acc)


def solution(mesh):
    both = P(BOTH)
    in_specs = (both,) * 10 + (P("col"),) * 2
    return jax.shard_map(local, mesh=mesh, in_specs=in_specs, out_specs=both, check_vma=False)
```

```python
import functools

import jax
import jax.numpy as jnp
from jax import lax
from jax.experimental import pallas as pl
from jax.experimental.pallas import tpu as pltpu
from jax.sharding import PartitionSpec as P

HIGHEST = lax.Precision.HIGHEST
BOTH = ("col", "sub")
SPARE = 16
VMEM = pl.BlockSpec(memory_space=pltpu.VMEM)
SMEM = pl.BlockSpec(memory_space=pltpu.SMEM)
HBM = pl.BlockSpec(memory_space=pltpu.HBM)


def call(body, ins, outs, scratch=(), mib=16, name=None):
    return pl.pallas_call(
        body,
        in_specs=ins,
        out_specs=[VMEM] * len(outs),
        out_shape=[jax.ShapeDtypeStruct(shape, kind) for shape, kind in outs],
        scratch_shapes=scratch,
        compiler_params=pltpu.CompilerParams(vmem_limit_bytes=mib * 2**20),
        cost_estimate=pl.CostEstimate(flops=0, bytes_accessed=0, transcendentals=0),
        name=name,
    )


def shift(value, step):
    count = lax.axis_size(BOTH)
    pairs = [(i, i + step) for i in range(count) if 0 <= i + step < count]
    return lax.ppermute(value, BOTH, pairs)


def exact(a, b, contract=(1, 0)):
    dims = (((contract[0],), (contract[1],)), ((), ()))
    return lax.dot_general(a, b, dims, precision=HIGHEST, preferred_element_type=jnp.float32)


def in_hbm(value):
    return pltpu.with_memory_space_constraint(value, pltpu.HBM)


def upward_body(*refs):
    sources, refs = refs[:6], refs[6:]
    (vec_ref, basis_ref, transfer_ref, cluster_ref, couple_ref, top_couple_ref), refs = refs[:6], refs[6:]
    (first_ref, second_ref, coefs_ref, packed_ref, low_ref, top_ref, sems) = refs
    leaves, rank, rows = basis_ref.shape
    pairs = list(zip(sources, (vec_ref, basis_ref, transfer_ref, cluster_ref, couple_ref, top_couple_ref)))
    pairs.append((sources[0].at[: first_ref.shape[0], :], first_ref))
    pairs.append((sources[0].at[vec_ref.shape[0] - second_ref.shape[0] :, :], second_ref))
    copies = [
        pltpu.make_async_copy(source, target, sems.at[i]) for i, (source, target) in enumerate(pairs)
    ]
    for copy in copies:
        copy.start()
    for copy in copies:
        copy.wait()
    for leaf in range(leaves):
        coefs_ref[leaf * rank : (leaf + 1) * rank, :] = jnp.dot(
            basis_ref[leaf], vec_ref[leaf * rows : (leaf + 1) * rows, :], preferred_element_type=jnp.float32
        )
    whole = coefs_ref[...]
    transfer = transfer_ref[...].reshape(leaves * rank, rank)
    cluster = exact(transfer, whole, (0, 0))
    low_ref[...] = cluster
    top_ref[0] = exact(cluster_ref[0], cluster, (0, 0))
    most = jnp.max(jnp.abs(whole), axis=(0, 1), keepdims=True)
    power = jnp.floor(jnp.log2(jnp.maximum(most, 1e-30)))
    packed_ref[: leaves * rank, :] = whole * jnp.exp2(14.0 - power)
    packed_ref[leaves * rank :, :] = jnp.broadcast_to(power, (SPARE, whole.shape[1]))


def upward(vectors, basis, transfer, cluster_transfer, cluster_coupling, top_coupling):
    leaves, rank, _ = basis.shape
    points, columns = vectors.shape
    f32 = jnp.float32
    arrays = (vectors, basis, transfer, cluster_transfer, cluster_coupling, top_coupling)
    return call(
        upward_body,
        [HBM] * 6,
        [(array.shape, array.dtype) for array in arrays]
        + [
            ((points // 2 + SPARE, columns), vectors.dtype),
            ((points // 2, columns), vectors.dtype),
            ((leaves * rank, columns), f32),
            ((leaves * rank + SPARE, columns), f32),
            ((rank, columns), f32),
            ((1, rank, columns), f32),
        ],
        scratch=[pltpu.SemaphoreType.DMA((8,))],
        name="leaf_and_cluster_coefs",
    )(*[in_hbm(array) for array in arrays])


def top_body(straight, partner_ref, coupling_ref, col_ref, low_ref, both_ref):
    col = lax.axis_index("col")
    top = None
    for k in range(coupling_ref.shape[1]):
        place = partner_ref[0, k]
        place = place if straight else lax.bitwise_xor(place, col)
        term = exact(coupling_ref[0, k], col_ref[place])
        top = term if top is None else top + term
    both_ref[0] = low_ref[...]
    both_ref[1] = top


def top_share(partner, coupling, cols, low):
    count = lax.axis_size("col")
    return call(
        functools.partial(top_body, bool(count & (count - 1))),
        [SMEM] + [VMEM] * 3,
        [((2,) + low.shape, jnp.float32)],
        name="top_field_share",
    )(partner, coupling, cols, low)[0]


def join_body(first_ref, second_ref, out_ref):
    width = first_ref.shape[0]
    out_ref[:width] = first_ref[...]
    out_ref[width:] = second_ref[...]


def join(first, second):
    shape = (2 * first.shape[0],) + first.shape[1:]
    return call(join_body, [VMEM] * 2, [(shape, first.dtype)], name="join_cols")(first, second)[0]


def gather_sub(value):
    count = lax.axis_size("sub")
    parts = [value]
    for step in range(1, count):
        pairs = [(i, (i + step) % count) for i in range(count)]
        parts.append(lax.ppermute(value, "sub", pairs))
    return parts


def gather_col(value):
    count = lax.axis_size("col")
    if count & (count - 1):
        return lax.all_gather(value, "col", axis=0, tiled=True)
    width = 1
    while width < count:
        pairs = [(i, i ^ width) for i in range(count)]
        value = join(value, lax.ppermute(value, "col", pairs))
        width *= 2
    return value


def far_body(far_ref, near_ref, coupling_in, low_ref, own_ref, high_ref, field_ref, coupling_ref, window, sems):
    leaves, slots, rank, _ = coupling_ref.shape
    rows = leaves * rank

    def copy(leaf):
        return pltpu.make_async_copy(coupling_in.at[leaf], coupling_ref.at[leaf], sems.at[leaf])

    @pl.loop(0, leaves)
    def _(leaf):
        copy(leaf).start()

    first = near_ref[0, 0] - leaves
    for place, ref in ((0, low_ref), (2, high_ref)):
        scale = jnp.exp2(ref[rows : rows + 1, :] - 14.0)
        window[place * rows : (place + 1) * rows, :] = ref[:rows, :] * scale
    window[rows : 2 * rows, :] = own_ref[...]

    @pl.loop(0, leaves)
    def _(leaf):
        copy(leaf).wait()
        picked = []
        for k in range(slots):
            place = jnp.clip(far_ref[k, leaf] - first, 0, 3 * leaves - 1)
            picked.append(window[pl.ds(pl.multiple_of(place * rank, rank), rank), :])
        here = coupling_ref[leaf]
        wide = jnp.concatenate([here[k] for k in range(slots)], axis=1)
        at = pl.ds(pl.multiple_of(leaf * rank, rank), rank)
        field_ref[at, :] = exact(wide, jnp.concatenate(picked, axis=0))


def far(leaf_far, near_index, coupling, low, own, high):
    leaves, _, rank, _ = coupling.shape
    return call(
        far_body,
        [SMEM] * 2 + [HBM] + [VMEM] * 3,
        [(own.shape, jnp.float32)],
        scratch=[
            pltpu.VMEM(coupling.shape, coupling.dtype),
            pltpu.VMEM((3 * leaves * rank, own.shape[1]), jnp.float32),
            pltpu.SemaphoreType.DMA((leaves,)),
        ],
        name="far_field_of_leaves",
    )(leaf_far, near_index, in_hbm(coupling), low, own, high)[0]


def down_body(subs, *refs):
    (partner_ref, near_ref), refs = refs[:2], refs[2:]
    part_refs, refs = refs[:subs], refs[subs:]
    (coupling_ref, cluster_ref, transfer_ref, field_ref, basis_ref, blocks_ref), refs = refs[:6], refs[6:]
    (own_ref, high_ref, acc_ref, held_ref, stack, window, sems) = refs
    leaves, rank, rows = basis_ref.shape
    slots = blocks_ref.shape[1]

    def copy(leaf):
        return pltpu.make_async_copy(blocks_ref.at[leaf], held_ref.at[leaf], sems.at[leaf])

    @pl.loop(0, leaves)
    def _(leaf):
        copy(leaf).start()

    sub = lax.axis_index("sub")
    top = None
    for j in range(subs):
        stack[j] = part_refs[j][0]
        top = part_refs[j][1] if top is None else top + part_refs[j][1]
    cluster = exact(cluster_ref[0], top)
    for k in range(coupling_ref.shape[1]):
        place = lax.rem(sub - partner_ref[0, k] + subs, subs)
        cluster = cluster + exact(coupling_ref[0, k], stack[place])
    transfer = transfer_ref[...].reshape(leaves * rank, rank)
    field_ref[...] += exact(transfer, cluster)

    window[: leaves * rows, :] = own_ref[...]
    window[leaves * rows : 2 * leaves * rows, :] = high_ref[...]
    window[2 * leaves * rows :, :] = jnp.zeros((rows, high_ref.shape[1]), window.dtype)
    first = near_ref[0, 0]

    @pl.loop(0, leaves)
    def _(leaf):
        copy(leaf).wait()
        field = field_ref[pl.ds(pl.multiple_of(leaf * rank, rank), rank), :].astype(jnp.bfloat16)
        acc = lax.dot_general(
            basis_ref[leaf], field, (((0,), (0,)), ((), ())), preferred_element_type=jnp.float32
        )
        for k in range(slots):
            place = near_ref[k, leaf] - first
            place = jnp.where(place < 0, 2 * leaves, jnp.minimum(place, 2 * leaves - 1))
            start = pl.multiple_of(place * rows, rows)
            acc = acc + jnp.dot(
                held_ref[leaf, k], window[pl.ds(start, rows), :], preferred_element_type=jnp.float32
            )
        acc_ref[pl.ds(pl.multiple_of(leaf * rows, rows), rows), :] = acc


def down(partner, near_index, parts, coupling, cluster_transfer, transfer, field, basis, blocks, own, high):
    leaves, rank, rows = basis.shape
    columns = high.shape[1]
    subs = len(parts)
    return call(
        functools.partial(down_body, subs),
        [SMEM] * 2 + [VMEM] * (subs + 5) + [HBM] + [VMEM] * 2,
        [(high.shape, jnp.float32), (blocks.shape, blocks.dtype)],
        scratch=[
            pltpu.VMEM((subs, rank, columns), jnp.float32),
            pltpu.VMEM(((2 * leaves + 1) * rows, columns), high.dtype),
            pltpu.SemaphoreType.DMA((leaves,)),
        ],
        mib=32,
        name="down_and_near_own_high",
    )(
        partner, near_index, *parts, coupling, cluster_transfer, transfer, field, basis, in_hbm(blocks), own, high,
    )


def last_body(near_ref, blocks_ref, low_first_ref, low_second_ref, acc_ref, out_ref, held, sem):
    leaves, slots, rows, _ = blocks_ref.shape
    first = near_ref[0, 0] - leaves
    split = leaves // 2

    def copy(leaf):
        here = pl.ds(pl.multiple_of(leaf * rows, rows), rows)
        return pltpu.make_async_copy(held.at[here, :], out_ref.at[here, :], sem)

    @pl.loop(0, leaves)
    def _(leaf):
        here = pl.ds(pl.multiple_of(leaf * rows, rows), rows)
        for k in range(1, slots):
            place = jnp.maximum(near_ref[k, leaf] - first, 0)

            def add(ref, at):
                start = pl.multiple_of(at * rows, rows)
                acc_ref[here, :] += jnp.dot(
                    blocks_ref[leaf, k], ref[pl.ds(start, rows), :], preferred_element_type=jnp.float32
                )

            pl.when(place < split)(lambda: add(low_first_ref, place))
            pl.when((place >= split) & (place < leaves))(lambda: add(low_second_ref, place - split))

        held[here, :] = acc_ref[here, :].astype(held.dtype)
        copy(leaf).start()

    pltpu.make_async_copy(held, out_ref, sem).wait()


def last(near_index, blocks, low_first, low_second, acc):
    return pl.pallas_call(
        last_body,
        in_specs=[SMEM] + [VMEM] * 4,
        out_specs=HBM,
        out_shape=jax.ShapeDtypeStruct(acc.shape, low_first.dtype),
        scratch_shapes=[pltpu.VMEM(acc.shape, low_first.dtype), pltpu.SemaphoreType.DMA],
        compiler_params=pltpu.CompilerParams(vmem_limit_bytes=32 * 2**20),
        cost_estimate=pl.CostEstimate(flops=0, bytes_accessed=0, transcendentals=0),
        name="near_low",
    )(near_index, blocks, low_first, low_second, acc)


def local(
    vectors,
    near_blocks,
    near_index,
    leaf_basis,
    leaf_transfer,
    leaf_coupling,
    leaf_far,
    cluster_transfer,
    cluster_coupling,
    cluster_partner,
    top_coupling,
    top_partner,
):
    high_vec = shift(vectors, -1)

    near_index, leaf_far = near_index.T, leaf_far.T
    own, basis, transfer, cluster, couple, top_couple, first, second, coefs, packed, low, top = upward(
        vectors, leaf_basis, leaf_transfer, cluster_transfer, cluster_coupling, top_coupling
    )
    halved = packed.astype(jnp.float16)
    low_half = shift(halved, 1)
    high_half = shift(halved, -1)
    share = top_share(top_partner, top_couple, gather_col(top), low)
    parts = gather_sub(share)

    first_sent, _ = lax.optimization_barrier((first, share))
    low_first = shift(first_sent, 1)
    second_sent, parts, low_half, high_half = lax.optimization_barrier((second, parts, low_half, high_half))
    low_second = shift(second_sent, 1)

    low_coefs = low_half.astype(jnp.float32)
    high_coefs = high_half.astype(jnp.float32)
    field = far(leaf_far, near_index, leaf_coupling, low_coefs, coefs, high_coefs)
    acc, blocks = down(
        cluster_partner, near_index, parts, couple, cluster, transfer, field, basis, near_blocks, own, high_vec
    )
    return last(near_index, blocks, low_first, low_second, acc)


def solution(mesh):
    both = P(BOTH)
    in_specs = (both,) * 10 + (P("col"),) * 2
    return jax.shard_map(local, mesh=mesh, in_specs=in_specs, out_specs=both, check_vma=False)
```

```python
import functools

import jax
import jax.numpy as jnp
from jax import lax
from jax.experimental import pallas as pl
from jax.experimental.pallas import tpu as pltpu
from jax.sharding import PartitionSpec as P

HIGHEST = lax.Precision.HIGHEST
BOTH = ("col", "sub")
SPARE = 16
VMEM = pl.BlockSpec(memory_space=pltpu.VMEM)
SMEM = pl.BlockSpec(memory_space=pltpu.SMEM)
HBM = pl.BlockSpec(memory_space=pltpu.HBM)


def call(body, ins, outs, scratch=(), mib=16, name=None):
    return pl.pallas_call(
        body,
        in_specs=ins,
        out_specs=[VMEM] * len(outs),
        out_shape=[jax.ShapeDtypeStruct(shape, kind) for shape, kind in outs],
        scratch_shapes=scratch,
        compiler_params=pltpu.CompilerParams(vmem_limit_bytes=mib * 2**20),
        cost_estimate=pl.CostEstimate(flops=0, bytes_accessed=0, transcendentals=0),
        name=name,
    )


def shift(value, step):
    count = lax.axis_size(BOTH)
    pairs = [(i, i + step) for i in range(count) if 0 <= i + step < count]
    return lax.ppermute(value, BOTH, pairs)


def exact(a, b, contract=(1, 0)):
    dims = (((contract[0],), (contract[1],)), ((), ()))
    return lax.dot_general(a, b, dims, precision=HIGHEST, preferred_element_type=jnp.float32)


def scale(value):
    most = jnp.max(jnp.abs(value), axis=(0, 1), keepdims=True)
    power = jnp.floor(jnp.log2(jnp.maximum(most, 1e-30)))
    return value * jnp.exp2(14.0 - power), power


def in_hbm(value):
    return pltpu.with_memory_space_constraint(value, pltpu.HBM)


def upward_body(*refs):
    sources, targets, refs = refs[:6], refs[6:12], refs[12:]
    vec_ref, basis_ref, transfer_ref, cluster_ref, _, _ = targets
    first_ref, second_ref, coefs_ref, long_ref, short_ref, pair_ref, sems = refs
    leaves, rank, rows = basis_ref.shape
    columns = vec_ref.shape[1]
    pairs = list(zip(sources, targets))
    pairs.append((sources[0].at[: first_ref.shape[0], :], first_ref))
    pairs.append((sources[0].at[vec_ref.shape[0] - second_ref.shape[0] :, :], second_ref))
    copies = [pltpu.make_async_copy(source, target, sems.at[i]) for i, (source, target) in enumerate(pairs)]
    for copy in copies:
        copy.start()
    for copy in copies:
        copy.wait()
    for leaf in range(leaves):
        coefs_ref[leaf * rank : (leaf + 1) * rank, :] = jnp.dot(
            basis_ref[leaf], vec_ref[leaf * rows : (leaf + 1) * rows, :], preferred_element_type=jnp.float32
        )
    whole = coefs_ref[...]
    transfer = transfer_ref[...].reshape(leaves * rank, rank)
    low = exact(transfer, whole, (0, 0))
    top = exact(cluster_ref[0], low, (0, 0))
    pair_ref[0] = low
    pair_ref[1] = top
    half = (SPARE // 2, columns)
    low, low_power = scale(low)
    top, top_power = scale(top)
    short_ref[:rank, :] = low
    short_ref[rank : 2 * rank, :] = top
    short_ref[2 * rank : 2 * rank + SPARE // 2, :] = jnp.broadcast_to(low_power, half)
    short_ref[2 * rank + SPARE // 2 :, :] = jnp.broadcast_to(top_power, half)
    whole, power = scale(whole)
    length = leaves * rank
    long_ref[:length, :] = whole
    long_ref[length : length + SPARE, :] = jnp.broadcast_to(power, (SPARE, columns))
    long_ref[length + SPARE :, :] = short_ref[...]


def upward(vectors, basis, transfer, cluster_transfer, cluster_coupling, top_coupling):
    leaves, rank, _ = basis.shape
    points, columns = vectors.shape
    f32 = jnp.float32
    arrays = (vectors, basis, transfer, cluster_transfer, cluster_coupling, top_coupling)
    short = 2 * rank + SPARE
    return call(
        upward_body,
        [HBM] * 6,
        [(array.shape, array.dtype) for array in arrays]
        + [
            ((points // 2 + SPARE, columns), vectors.dtype),
            ((points // 2, columns), vectors.dtype),
            ((leaves * rank, columns), f32),
            ((leaves * rank + SPARE + short, columns), f32),
            ((short, columns), f32),
            ((2, rank, columns), f32),
        ],
        scratch=[pltpu.SemaphoreType.DMA((8,))],
        name="leaf_and_cluster_coefs",
    )(*[in_hbm(array) for array in arrays])


def cluster_body(subs, own_ref, low_ref, high_ref, *refs):
    part_refs, (stack_ref, top_ref) = refs[:-2], refs[-2:]
    rank = own_ref.shape[1]
    sub = lax.axis_index("sub")
    tops = [own_ref[1]]

    def put(valid, place, ref):
        at = ref.shape[0] - 2 * rank - SPARE
        values = []
        for i in range(2):
            power = ref[at + 2 * rank + i * SPARE // 2 : at + 2 * rank + i * SPARE // 2 + 1, :]
            values.append(ref[at + i * rank : at + (i + 1) * rank, :] * jnp.exp2(power - 14.0))

        @pl.when(valid)
        def _():
            stack_ref[place] = values[0]

        tops.append(jnp.where(valid, values[1], 0.0))

    stack_ref[sub] = own_ref[0]
    put(sub > 0, sub - 1, low_ref)
    put(sub < subs - 1, sub + 1, high_ref)
    for i, ref in enumerate(part_refs[:-1]):
        put(sub >= 0, lax.rem(sub - 2 - i + subs, subs), ref)
    if part_refs:
        put((sub == 0) | (sub == subs - 1), subs - 1 - sub, part_refs[-1])
    top_ref[0] = functools.reduce(jnp.add, tops)


def cluster_sums(own, low, high, parts):
    _, rank, columns = own.shape
    subs = lax.axis_size("sub")
    return call(
        functools.partial(cluster_body, subs),
        [VMEM] * (3 + len(parts)),
        [((subs, rank, columns), jnp.float32), ((1, rank, columns), jnp.float32)],
        name="sums_over_sub",
    )(own, low, high, *parts)


def join_body(first_ref, second_ref, out_ref):
    width = first_ref.shape[0]
    out_ref[:width] = first_ref[...]
    out_ref[width:] = second_ref[...]


def join(first, second):
    shape = (2 * first.shape[0],) + first.shape[1:]
    return call(join_body, [VMEM] * 2, [(shape, first.dtype)], name="join_cols")(first, second)[0]


def gather_sub(value):
    count = lax.axis_size("sub")
    parts = []
    for step in range(2, count - 1):
        pairs = [(i, (i + step) % count) for i in range(count)]
        parts.append(lax.ppermute(value, "sub", pairs))
    if count > 2:
        parts.append(lax.ppermute(value, "sub", [(0, count - 1), (count - 1, 0)]))
    return parts


def gather_col(value):
    count = lax.axis_size("col")
    if count & (count - 1):
        return lax.all_gather(value, "col", axis=0, tiled=True)
    width = 1
    while width < count:
        pairs = [(i, i ^ width) for i in range(count)]
        value = join(value, lax.ppermute(value, "col", pairs))
        width *= 2
    return value


def far_body(far_ref, near_ref, coupling_in, low_ref, own_ref, high_ref, field_ref, coupling_ref, window, sems):
    leaves, slots, rank, _ = coupling_ref.shape
    rows = leaves * rank

    def copy(leaf):
        return pltpu.make_async_copy(coupling_in.at[leaf], coupling_ref.at[leaf], sems.at[leaf])

    @pl.loop(0, leaves)
    def _(leaf):
        copy(leaf).start()

    first = near_ref[0, 0] - leaves
    for place, ref in ((0, low_ref), (2, high_ref)):
        scale = jnp.exp2(ref[rows : rows + 1, :] - 14.0)
        window[place * rows : (place + 1) * rows, :] = ref[:rows, :] * scale
    window[rows : 2 * rows, :] = own_ref[...]

    @pl.loop(0, leaves)
    def _(leaf):
        copy(leaf).wait()
        picked = []
        for k in range(slots):
            place = jnp.clip(far_ref[k, leaf] - first, 0, 3 * leaves - 1)
            picked.append(window[pl.ds(pl.multiple_of(place * rank, rank), rank), :])
        here = coupling_ref[leaf]
        wide = jnp.concatenate([here[k] for k in range(slots)], axis=1)
        at = pl.ds(pl.multiple_of(leaf * rank, rank), rank)
        field_ref[at, :] = exact(wide, jnp.concatenate(picked, axis=0))


def far(leaf_far, near_index, coupling, low, own, high):
    leaves, _, rank, _ = coupling.shape
    return call(
        far_body,
        [SMEM] * 2 + [HBM] + [VMEM] * 3,
        [(own.shape, jnp.float32)],
        scratch=[
            pltpu.VMEM(coupling.shape, coupling.dtype),
            pltpu.VMEM((3 * leaves * rank, own.shape[1]), jnp.float32),
            pltpu.SemaphoreType.DMA((leaves,)),
        ],
        name="far_field_of_leaves",
    )(leaf_far, near_index, in_hbm(coupling), low, own, high)[0]


def near_body(near_ref, blocks_ref, own_ref, high_ref, acc_ref, held_ref, window, sems):
    leaves, slots, rows, _ = blocks_ref.shape

    def copy(leaf):
        return pltpu.make_async_copy(blocks_ref.at[leaf], held_ref.at[leaf], sems.at[leaf])

    @pl.loop(0, leaves)
    def _(leaf):
        copy(leaf).start()

    window[: leaves * rows, :] = own_ref[...]
    window[leaves * rows : 2 * leaves * rows, :] = high_ref[...]
    window[2 * leaves * rows :, :] = jnp.zeros((rows, high_ref.shape[1]), window.dtype)
    first = near_ref[0, 0]

    @pl.loop(0, leaves)
    def _(leaf):
        copy(leaf).wait()
        acc = None
        for k in range(slots):
            place = near_ref[k, leaf] - first
            place = jnp.where(place < 0, 2 * leaves, jnp.minimum(place, 2 * leaves - 1))
            start = pl.multiple_of(place * rows, rows)
            term = jnp.dot(
                held_ref[leaf, k], window[pl.ds(start, rows), :], preferred_element_type=jnp.float32
            )
            acc = term if acc is None else acc + term
        acc_ref[pl.ds(pl.multiple_of(leaf * rows, rows), rows), :] = acc


def near(near_index, blocks, own, high):
    leaves, _, rows, _ = blocks.shape
    return call(
        near_body,
        [SMEM, HBM, VMEM, VMEM],
        [(own.shape, jnp.float32), (blocks.shape, blocks.dtype)],
        scratch=[
            pltpu.VMEM(((2 * leaves + 1) * rows, own.shape[1]), own.dtype),
            pltpu.SemaphoreType.DMA((leaves,)),
        ],
        mib=32,
        name="near_own_and_high",
    )(near_index, in_hbm(blocks), own, high)


def down_body(
    straight, partner_ref, top_partner_ref, stack_ref, cols_ref, coupling_ref, top_coupling_ref, cluster_ref,
    transfer_ref, field_ref, basis_ref, acc_ref, out_ref, fields,
):
    leaves, rank, rows = basis_ref.shape
    col = lax.axis_index("col")
    top = None
    for k in range(top_coupling_ref.shape[1]):
        place = top_partner_ref[0, k]
        place = place if straight else lax.bitwise_xor(place, col)
        term = exact(top_coupling_ref[0, k], cols_ref[place])
        top = term if top is None else top + term
    cluster = exact(cluster_ref[0], top)
    for k in range(coupling_ref.shape[1]):
        cluster = cluster + exact(coupling_ref[0, k], stack_ref[partner_ref[0, k]])
    transfer = transfer_ref[...].reshape(leaves * rank, rank)
    fields[...] = (field_ref[...] + exact(transfer, cluster)).astype(fields.dtype)
    for leaf in range(leaves):
        here = slice(leaf * rows, (leaf + 1) * rows)
        out_ref[here, :] = acc_ref[here, :] + lax.dot_general(
            basis_ref[leaf],
            fields[leaf * rank : (leaf + 1) * rank, :],
            (((0,), (0,)), ((), ())),
            preferred_element_type=jnp.float32,
        )


def down(partner, top_partner, stack, cols, coupling, top_coupling, cluster_transfer, transfer, field, basis, acc):
    count = lax.axis_size("col")
    return call(
        functools.partial(down_body, bool(count & (count - 1))),
        [SMEM] * 2 + [VMEM] * 9,
        [(acc.shape, jnp.float32)],
        scratch=[pltpu.VMEM(field.shape, jnp.bfloat16)],
        name="fields_down",
    )(partner, top_partner, stack, cols, coupling, top_coupling, cluster_transfer, transfer, field, basis, acc)[0]


def last_body(near_ref, blocks_ref, low_first_ref, low_second_ref, acc_ref, out_ref, held, sem):
    leaves, slots, rows, _ = blocks_ref.shape
    split = leaves // 2
    first = near_ref[0, 0] - leaves

    def copy(leaf):
        here = pl.ds(pl.multiple_of(leaf * rows, rows), rows)
        return pltpu.make_async_copy(held.at[here, :], out_ref.at[here, :], sem)

    @pl.loop(0, leaves)
    def _(leaf):
        here = pl.ds(pl.multiple_of(leaf * rows, rows), rows)
        for k in range(1, slots):
            place = jnp.maximum(near_ref[k, leaf] - first, 0)

            def add(ref, at):
                start = pl.multiple_of(at * rows, rows)
                acc_ref[here, :] += jnp.dot(
                    blocks_ref[leaf, k], ref[pl.ds(start, rows), :], preferred_element_type=jnp.float32
                )

            pl.when(place < split)(lambda: add(low_first_ref, place))
            pl.when((place >= split) & (place < leaves))(lambda: add(low_second_ref, place - split))

        held[here, :] = acc_ref[here, :].astype(held.dtype)
        copy(leaf).start()

    pltpu.make_async_copy(held, out_ref, sem).wait()


def last(near_index, blocks, low_first, low_second, acc):
    return pl.pallas_call(
        last_body,
        in_specs=[SMEM] + [VMEM] * 4,
        out_specs=HBM,
        out_shape=jax.ShapeDtypeStruct(acc.shape, low_first.dtype),
        scratch_shapes=[pltpu.VMEM(acc.shape, low_first.dtype), pltpu.SemaphoreType.DMA],
        compiler_params=pltpu.CompilerParams(vmem_limit_bytes=32 * 2**20),
        cost_estimate=pl.CostEstimate(flops=0, bytes_accessed=0, transcendentals=0),
        name="near_low",
    )(near_index, blocks, low_first, low_second, acc)


def local(
    vectors,
    near_blocks,
    near_index,
    leaf_basis,
    leaf_transfer,
    leaf_coupling,
    leaf_far,
    cluster_transfer,
    cluster_coupling,
    cluster_partner,
    top_coupling,
    top_partner,
):
    high_vec = shift(vectors, -1)
    near_index, leaf_far = near_index.T, leaf_far.T

    own, basis, transfer, cluster, couple, top_couple, first, second, coefs, long, short, pair = upward(
        vectors, leaf_basis, leaf_transfer, cluster_transfer, cluster_coupling, top_coupling
    )
    long, short = long.astype(jnp.float16), short.astype(jnp.float16)
    low_part = shift(long, 1)
    high_part = shift(long, -1)
    parts = gather_sub(short)
    first, high_vec, _ = lax.optimization_barrier((first, high_vec, long))
    low_first = shift(first, 1)
    acc, blocks = near(near_index, near_blocks, own, high_vec)

    second, parts, low_part, high_part, acc = lax.optimization_barrier((second, parts, low_part, high_part, acc))
    low_second = shift(second, 1)

    parts = [part.astype(jnp.float32) for part in parts]
    low_part, high_part = low_part.astype(jnp.float32), high_part.astype(jnp.float32)
    stack, top = cluster_sums(pair, low_part, high_part, parts)
    cols = gather_col(top)
    field = far(leaf_far, near_index, leaf_coupling, low_part, coefs, high_part)
    acc = down(
        cluster_partner, top_partner, stack, cols, couple, top_couple, cluster, transfer, field, basis, acc
    )
    return last(near_index, blocks, low_first, low_second, acc)


def solution(mesh):
    both = P(BOTH)
    in_specs = (both,) * 10 + (P("col"),) * 2
    return jax.shard_map(local, mesh=mesh, in_specs=in_specs, out_specs=both, check_vma=False)
```

```python
import functools

import jax
import jax.numpy as jnp
from jax import lax
from jax.experimental import pallas as pl
from jax.experimental.pallas import tpu as pltpu
from jax.sharding import PartitionSpec as P

HIGHEST = lax.Precision.HIGHEST
BOTH = ("col", "sub")
SPARE = 16
GROUP = 4
BATCH = 8
VMEM = pl.BlockSpec(memory_space=pltpu.VMEM)
SMEM = pl.BlockSpec(memory_space=pltpu.SMEM)
HBM = pl.BlockSpec(memory_space=pltpu.HBM)


def call(body, ins, outs, scratch=(), mib=16, name=None):
    return pl.pallas_call(
        body,
        in_specs=ins,
        out_specs=[VMEM] * len(outs),
        out_shape=[jax.ShapeDtypeStruct(shape, kind) for shape, kind in outs],
        scratch_shapes=scratch,
        compiler_params=pltpu.CompilerParams(vmem_limit_bytes=mib * 2**20),
        cost_estimate=pl.CostEstimate(flops=0, bytes_accessed=0, transcendentals=0),
        name=name,
    )


def shift(value, step):
    count = lax.axis_size(BOTH)
    pairs = [(i, i + step) for i in range(count) if 0 <= i + step < count]
    return lax.ppermute(value, BOTH, pairs)


def exact(a, b, contract=(1, 0)):
    dims = (((contract[0],), (contract[1],)), ((), ()))
    return lax.dot_general(a, b, dims, precision=HIGHEST, preferred_element_type=jnp.float32)


def scale(value):
    most = jnp.max(jnp.abs(value), axis=(0, 1), keepdims=True)
    power = jnp.floor(jnp.log2(jnp.maximum(most, 1e-30)))
    return value * jnp.exp2(14.0 - power), power


def in_hbm(value):
    return pltpu.with_memory_space_constraint(value, pltpu.HBM)


def upward_body(*refs):
    sources, targets, refs = refs[:6], refs[6:12], refs[12:]
    vec_ref, basis_ref, transfer_ref, cluster_ref, _, _ = targets
    first_ref, second_ref, coefs_ref, long_ref, short_ref, pair_ref, sems = refs
    leaves, rank, rows = basis_ref.shape
    columns = vec_ref.shape[1]
    pairs = list(zip(sources, targets))
    pairs.append((sources[0].at[: first_ref.shape[0], :], first_ref))
    pairs.append((sources[0].at[vec_ref.shape[0] - second_ref.shape[0] :, :], second_ref))
    copies = [pltpu.make_async_copy(source, target, sems.at[i]) for i, (source, target) in enumerate(pairs)]
    for copy in copies:
        copy.start()
    for copy in copies:
        copy.wait()
    for leaf in range(leaves):
        coefs_ref[leaf * rank : (leaf + 1) * rank, :] = jnp.dot(
            basis_ref[leaf], vec_ref[leaf * rows : (leaf + 1) * rows, :], preferred_element_type=jnp.float32
        )
    whole = coefs_ref[...]
    transfer = transfer_ref[...].reshape(leaves * rank, rank)
    low = exact(transfer, whole, (0, 0))
    top = exact(cluster_ref[0], low, (0, 0))
    pair_ref[0] = low
    pair_ref[1] = top
    half = (SPARE // 2, columns)
    low, low_power = scale(low)
    top, top_power = scale(top)
    short_ref[:rank, :] = low
    short_ref[rank : 2 * rank, :] = top
    short_ref[2 * rank : 2 * rank + SPARE // 2, :] = jnp.broadcast_to(low_power, half)
    short_ref[2 * rank + SPARE // 2 :, :] = jnp.broadcast_to(top_power, half)
    whole, power = scale(whole)
    length = leaves * rank
    long_ref[:length, :] = whole
    long_ref[length : length + SPARE, :] = jnp.broadcast_to(power, (SPARE, columns))
    long_ref[length + SPARE :, :] = short_ref[...]


def upward(vectors, basis, transfer, cluster_transfer, cluster_coupling, top_coupling):
    leaves, rank, _ = basis.shape
    points, columns = vectors.shape
    f32 = jnp.float32
    arrays = (vectors, basis, transfer, cluster_transfer, cluster_coupling, top_coupling)
    short = 2 * rank + SPARE
    return call(
        upward_body,
        [HBM] * 6,
        [(array.shape, array.dtype) for array in arrays]
        + [
            ((points // 2 + SPARE, columns), vectors.dtype),
            ((points // 2, columns), vectors.dtype),
            ((leaves * rank, columns), f32),
            ((leaves * rank + SPARE + short, columns), f32),
            ((short, columns), f32),
            ((2, rank, columns), f32),
        ],
        scratch=[pltpu.SemaphoreType.DMA((8,))],
        name="leaf_and_cluster_coefs",
    )(*[in_hbm(array) for array in arrays])


def cluster_body(subs, own_ref, low_ref, high_ref, *refs):
    part_refs, (stack_ref, top_ref) = refs[:-2], refs[-2:]
    rank = own_ref.shape[1]
    sub = lax.axis_index("sub")
    tops = [own_ref[1]]

    def put(valid, place, ref):
        at = ref.shape[0] - 2 * rank - SPARE
        values = []
        for i in range(2):
            power = ref[at + 2 * rank + i * SPARE // 2 : at + 2 * rank + i * SPARE // 2 + 1, :]
            values.append(ref[at + i * rank : at + (i + 1) * rank, :] * jnp.exp2(power - 14.0))

        @pl.when(valid)
        def _():
            stack_ref[place] = values[0]

        tops.append(jnp.where(valid, values[1], 0.0))

    stack_ref[sub] = own_ref[0]
    put(sub > 0, sub - 1, low_ref)
    put(sub < subs - 1, sub + 1, high_ref)
    for i, ref in enumerate(part_refs[:-1]):
        put(sub >= 0, lax.rem(sub - 2 - i + subs, subs), ref)
    if part_refs:
        put((sub == 0) | (sub == subs - 1), subs - 1 - sub, part_refs[-1])
    top_ref[0] = functools.reduce(jnp.add, tops)


def cluster_sums(own, low, high, parts):
    _, rank, columns = own.shape
    subs = lax.axis_size("sub")
    return call(
        functools.partial(cluster_body, subs),
        [VMEM] * (3 + len(parts)),
        [((subs, rank, columns), jnp.float32), ((1, rank, columns), jnp.float32)],
        name="sums_over_sub",
    )(own, low, high, *parts)


def join_body(first_ref, second_ref, out_ref):
    width = first_ref.shape[0]
    out_ref[:width] = first_ref[...]
    out_ref[width:] = second_ref[...]


def join(first, second):
    shape = (2 * first.shape[0],) + first.shape[1:]
    return call(join_body, [VMEM] * 2, [(shape, first.dtype)], name="join_cols")(first, second)[0]


def gather_sub(value):
    count = lax.axis_size("sub")
    parts = []
    for step in range(2, count - 1):
        pairs = [(i, (i + step) % count) for i in range(count)]
        parts.append(lax.ppermute(value, "sub", pairs))
    if count > 2:
        parts.append(lax.ppermute(value, "sub", [(0, count - 1), (count - 1, 0)]))
    return parts


def gather_col(value):
    count = lax.axis_size("col")
    if count & (count - 1):
        return lax.all_gather(value, "col", axis=0, tiled=True)
    width = 1
    while width < count:
        pairs = [(i, i ^ width) for i in range(count)]
        value = join(value, lax.ppermute(value, "col", pairs))
        width *= 2
    return value


def far_body(far_ref, near_ref, coupling_in, low_ref, own_ref, high_ref, field_ref, coupling_ref, window, sems):
    leaves, slots, rank, _ = coupling_ref.shape
    rows = leaves * rank

    def copy(leaf):
        return pltpu.make_async_copy(coupling_in.at[leaf], coupling_ref.at[leaf], sems.at[leaf])

    @pl.loop(0, leaves)
    def _(leaf):
        copy(leaf).start()

    first = near_ref[0, 0] - leaves
    for place, ref in ((0, low_ref), (2, high_ref)):
        scale = jnp.exp2(ref[rows : rows + 1, :] - 14.0)
        window[place * rows : (place + 1) * rows, :] = ref[:rows, :] * scale
    window[rows : 2 * rows, :] = own_ref[...]

    for leaf in range(leaves):
        copy(leaf).wait()
    for leaf in range(leaves):
        picked = []
        for k in range(slots):
            place = jnp.clip(far_ref[k, leaf] - first, 0, 3 * leaves - 1)
            picked.append(window[pl.ds(pl.multiple_of(place * rank, rank), rank), :])
        here = coupling_ref[leaf]
        wide = jnp.concatenate([here[k] for k in range(slots)], axis=1)
        field_ref[leaf * rank : (leaf + 1) * rank, :] = exact(wide, jnp.concatenate(picked, axis=0))


def far(leaf_far, near_index, coupling, low, own, high):
    leaves, _, rank, _ = coupling.shape
    return call(
        far_body,
        [SMEM] * 2 + [HBM] + [VMEM] * 3,
        [(own.shape, jnp.float32)],
        scratch=[
            pltpu.VMEM(coupling.shape, coupling.dtype),
            pltpu.VMEM((3 * leaves * rank, own.shape[1]), jnp.float32),
            pltpu.SemaphoreType.DMA((leaves,)),
        ],
        name="far_field_of_leaves",
    )(leaf_far, near_index, in_hbm(coupling), low, own, high)[0]


def near_body(near_ref, blocks_ref, own_ref, high_ref, acc_ref, held_ref, list_ref, window, sems):
    leaves, slots, rows, _ = blocks_ref.shape

    def copy(leaf):
        return pltpu.make_async_copy(blocks_ref.at[leaf], held_ref.at[leaf], sems.at[leaf])

    for leaf in range(leaves):
        copy(leaf).start()

    window[: leaves * rows, :] = own_ref[...]
    window[leaves * rows : 2 * leaves * rows, :] = high_ref[...]
    window[2 * leaves * rows :, :] = jnp.zeros((rows, high_ref.shape[1]), window.dtype)
    first = near_ref[0, 0]
    room = list_ref.shape[1]

    @pl.loop(0, room)
    def _(i):
        for row in range(4):
            list_ref[row, i] = 0

    half = leaves // 2

    def note(leaf, counts):
        found = jnp.int32(0)
        for k in range(1, slots):
            place = near_ref[k, leaf] - first + leaves
            after = []
            for i, valid in enumerate((place < half, (place >= half) & (place < leaves))):

                @pl.when(valid)
                def _(i=i, place=place, k=k, count=counts[i]):
                    list_ref[2 * i, count] = leaf * slots + k
                    list_ref[2 * i + 1, count] = jnp.maximum(place - i * half, 0)

                after.append(counts[i] + valid.astype(jnp.int32))
                found = found + valid.astype(jnp.int32)
            counts = tuple(after)
        list_ref[4, leaf] = found
        return counts

    counts = lax.fori_loop(0, leaves, note, (jnp.int32(0), jnp.int32(0)))
    list_ref[5, 0] = counts[0]
    list_ref[5, 1] = counts[1]

    for group in range(0, leaves, GROUP):
        for leaf in range(group, group + GROUP):
            copy(leaf).wait()
        for leaf in range(group, group + GROUP):
            acc = None
            for k in range(slots):
                place = near_ref[k, leaf] - first
                place = jnp.where(place < 0, 2 * leaves, jnp.minimum(place, 2 * leaves - 1))
                start = pl.multiple_of(place * rows, rows)
                term = jnp.dot(
                    held_ref[leaf, k], window[pl.ds(start, rows), :], preferred_element_type=jnp.float32
                )
                acc = term if acc is None else acc + term
            acc_ref[leaf * rows : (leaf + 1) * rows, :] = acc


def near(near_index, blocks, own, high):
    leaves, slots, rows, _ = blocks.shape
    room = leaves * slots + BATCH
    return pl.pallas_call(
        near_body,
        in_specs=[SMEM, HBM, VMEM, VMEM],
        out_specs=[VMEM, VMEM, SMEM],
        out_shape=[
            jax.ShapeDtypeStruct(own.shape, jnp.float32),
            jax.ShapeDtypeStruct(blocks.shape, blocks.dtype),
            jax.ShapeDtypeStruct((6, room), jnp.int32),
        ],
        scratch_shapes=[
            pltpu.VMEM(((2 * leaves + 1) * rows, own.shape[1]), own.dtype),
            pltpu.SemaphoreType.DMA((leaves,)),
        ],
        compiler_params=pltpu.CompilerParams(vmem_limit_bytes=32 * 2**20),
        cost_estimate=pl.CostEstimate(flops=0, bytes_accessed=0, transcendentals=0),
        name="near_own_and_high",
    )(near_index, in_hbm(blocks), own, high)


def down_body(
    straight, partner_ref, top_partner_ref, stack_ref, cols_ref, coupling_ref, top_coupling_ref, cluster_ref,
    transfer_ref, field_ref, basis_ref, acc_ref, sum_ref, out_ref, fields, held, sem,
):
    leaves, rank, rows = basis_ref.shape
    col = lax.axis_index("col")
    top = None
    for k in range(top_coupling_ref.shape[1]):
        place = top_partner_ref[0, k]
        place = place if straight else lax.bitwise_xor(place, col)
        term = exact(top_coupling_ref[0, k], cols_ref[place])
        top = term if top is None else top + term
    cluster = exact(cluster_ref[0], top)
    for k in range(coupling_ref.shape[1]):
        cluster = cluster + exact(coupling_ref[0, k], stack_ref[partner_ref[0, k]])
    transfer = transfer_ref[...].reshape(leaves * rank, rank)
    fields[...] = (field_ref[...] + exact(transfer, cluster)).astype(fields.dtype)
    for leaf in range(leaves):
        here = slice(leaf * rows, (leaf + 1) * rows)
        total = acc_ref[here, :] + lax.dot_general(
            basis_ref[leaf],
            fields[leaf * rank : (leaf + 1) * rank, :],
            (((0,), (0,)), ((), ())),
            preferred_element_type=jnp.float32,
        )
        sum_ref[here, :] = total
        held[here, :] = total.astype(held.dtype)
    copy = pltpu.make_async_copy(held, out_ref, sem)
    copy.start()
    copy.wait()


def down(partner, top_partner, stack, cols, coupling, top_coupling, cluster_transfer, transfer, field, basis, acc):
    count = lax.axis_size("col")
    return pl.pallas_call(
        functools.partial(down_body, bool(count & (count - 1))),
        in_specs=[SMEM] * 2 + [VMEM] * 9,
        out_specs=[VMEM, HBM],
        out_shape=[jax.ShapeDtypeStruct(acc.shape, jnp.float32), pltpu.HBM(acc.shape, jnp.bfloat16)],
        scratch_shapes=[
            pltpu.VMEM(field.shape, jnp.bfloat16),
            pltpu.VMEM(acc.shape, jnp.bfloat16),
            pltpu.SemaphoreType.DMA,
        ],
        compiler_params=pltpu.CompilerParams(vmem_limit_bytes=16 * 2**20),
        cost_estimate=pl.CostEstimate(flops=0, bytes_accessed=0, transcendentals=0),
        name="fields_down",
    )(partner, top_partner, stack, cols, coupling, top_coupling, cluster_transfer, transfer, field, basis, acc)


def add_listed(list_ref, part, blocks_ref, low_ref, acc_ref):
    _, slots, rows, _ = blocks_ref.shape
    count = list_ref[5, part]

    @pl.loop(0, pl.cdiv(count, BATCH))
    def _(batch):
        terms = []
        for i in range(BATCH):
            at = list_ref[2 * part, batch * BATCH + i]
            start = pl.multiple_of(list_ref[2 * part + 1, batch * BATCH + i] * rows, rows)
            block = blocks_ref[at // slots, lax.rem(at, slots)]
            terms.append(jnp.dot(block, low_ref[pl.ds(start, rows), :], preferred_element_type=jnp.float32))
        for i in range(BATCH):
            at = batch * BATCH + i

            @pl.when(at < count)
            def _(i=i, at=at):
                start = pl.multiple_of(list_ref[2 * part, at] // slots * rows, rows)
                acc_ref[pl.ds(start, rows), :] += terms[i]


def low_body(list_ref, blocks_ref, low_ref, acc_in, acc_ref):
    add_listed(list_ref, 0, blocks_ref, low_ref, acc_ref)


def near_low(places, blocks, low, acc):
    return pl.pallas_call(
        low_body,
        in_specs=[SMEM] + [VMEM] * 3,
        out_specs=VMEM,
        out_shape=jax.ShapeDtypeStruct(acc.shape, acc.dtype),
        input_output_aliases={3: 0},
        compiler_params=pltpu.CompilerParams(vmem_limit_bytes=16 * 2**20),
        cost_estimate=pl.CostEstimate(flops=0, bytes_accessed=0, transcendentals=0),
        name="near_low_first",
    )(places, blocks, low, acc)


def last_body(list_ref, blocks_ref, low_ref, acc_ref, out_in, out_ref, held, sems):
    leaves, _, rows, _ = blocks_ref.shape
    add_listed(list_ref, 1, blocks_ref, low_ref, acc_ref)

    def copy(leaf):
        here = slice(leaf * rows, (leaf + 1) * rows)
        return pltpu.make_async_copy(held.at[here, :], out_ref.at[here, :], sems.at[leaf])

    for leaf in range(leaves):

        @pl.when(list_ref[4, leaf] > 0)
        def _(leaf=leaf):
            here = slice(leaf * rows, (leaf + 1) * rows)
            held[here, :] = acc_ref[here, :].astype(held.dtype)
            copy(leaf).start()

    for leaf in range(leaves):

        @pl.when(list_ref[4, leaf] > 0)
        def _(leaf=leaf):
            copy(leaf).wait()


def last(places, blocks, low, acc, out):
    leaves = blocks.shape[0]
    return pl.pallas_call(
        last_body,
        in_specs=[SMEM] + [VMEM] * 3 + [HBM],
        out_specs=HBM,
        out_shape=jax.ShapeDtypeStruct(out.shape, out.dtype),
        input_output_aliases={4: 0},
        scratch_shapes=[
            pltpu.VMEM(out.shape, out.dtype),
            pltpu.SemaphoreType.DMA((leaves,)),
        ],
        compiler_params=pltpu.CompilerParams(vmem_limit_bytes=32 * 2**20),
        cost_estimate=pl.CostEstimate(flops=0, bytes_accessed=0, transcendentals=0),
        name="near_low_second",
    )(places, blocks, low, acc, out)


def local(
    vectors,
    near_blocks,
    near_index,
    leaf_basis,
    leaf_transfer,
    leaf_coupling,
    leaf_far,
    cluster_transfer,
    cluster_coupling,
    cluster_partner,
    top_coupling,
    top_partner,
):
    high_vec = shift(vectors, -1)
    near_index, leaf_far = near_index.T, leaf_far.T

    own, basis, transfer, cluster, couple, top_couple, first, second, coefs, long, short, pair = upward(
        vectors, leaf_basis, leaf_transfer, cluster_transfer, cluster_coupling, top_coupling
    )
    long, short = long.astype(jnp.float16), short.astype(jnp.float16)
    low_part = shift(long, 1)
    high_part = shift(long, -1)
    parts = gather_sub(short)
    first, high_vec, _ = lax.optimization_barrier((first, high_vec, long))
    low_first = shift(first, 1)
    acc, blocks, places = near(near_index, near_blocks, own, high_vec)

    second, parts, low_part, high_part, acc = lax.optimization_barrier((second, parts, low_part, high_part, acc))
    low_second = shift(second, 1)

    parts = [part.astype(jnp.float32) for part in parts]
    low_part, high_part = low_part.astype(jnp.float32), high_part.astype(jnp.float32)
    stack, top = cluster_sums(pair, low_part, high_part, parts)
    cols = gather_col(top)
    field = far(leaf_far, near_index, leaf_coupling, low_part, coefs, high_part)
    acc, out = down(
        cluster_partner, top_partner, stack, cols, couple, top_couple, cluster, transfer, field, basis, acc
    )
    acc = near_low(places, blocks, low_first, acc)
    return last(places, blocks, low_second, acc, out)


def solution(mesh):
    both = P(BOTH)
    in_specs = (both,) * 10 + (P("col"),) * 2
    return jax.shard_map(local, mesh=mesh, in_specs=in_specs, out_specs=both, check_vma=False)
```

```python
import functools

import jax
import jax.numpy as jnp
from jax import lax
from jax.experimental import pallas as pl
from jax.experimental.pallas import tpu as pltpu
from jax.sharding import PartitionSpec as P

HIGHEST = lax.Precision.HIGHEST
BOTH = ("col", "sub")
SPARE = 16
GROUP = 4
BATCH = 8
VMEM = pl.BlockSpec(memory_space=pltpu.VMEM)
SMEM = pl.BlockSpec(memory_space=pltpu.SMEM)
HBM = pl.BlockSpec(memory_space=pltpu.HBM)


def call(body, ins, outs, scratch=(), mib=16, name=None):
    return pl.pallas_call(
        body,
        in_specs=ins,
        out_specs=[VMEM] * len(outs),
        out_shape=[jax.ShapeDtypeStruct(shape, kind) for shape, kind in outs],
        scratch_shapes=scratch,
        compiler_params=pltpu.CompilerParams(vmem_limit_bytes=mib * 2**20),
        cost_estimate=pl.CostEstimate(flops=0, bytes_accessed=0, transcendentals=0),
        name=name,
    )


def shift(value, step):
    count = lax.axis_size(BOTH)
    pairs = [(i, i + step) for i in range(count) if 0 <= i + step < count]
    return lax.ppermute(value, BOTH, pairs)


def shift_around(value, by):
    count = lax.axis_size(BOTH)
    return lax.ppermute(value, BOTH, [(i, (i + by) % count) for i in range(count)])


def exact(a, b, contract=(1, 0)):
    dims = (((contract[0],), (contract[1],)), ((), ()))
    return lax.dot_general(a, b, dims, precision=HIGHEST, preferred_element_type=jnp.float32)


def scale(value):
    most = jnp.max(jnp.abs(value), axis=(0, 1), keepdims=True)
    power = jnp.floor(jnp.log2(jnp.maximum(most, 1e-30)))
    return value * jnp.exp2(14.0 - power), power


def in_hbm(value):
    return pltpu.with_memory_space_constraint(value, pltpu.HBM)


def upward_body(*refs):
    sources, targets, refs = refs[:6], refs[6:12], refs[12:]
    vec_ref, basis_ref, transfer_ref, cluster_ref, _, _ = targets
    first_ref, second_ref, coefs_ref, long_ref, short_ref, pair_ref, sems = refs
    leaves, rank, rows = basis_ref.shape
    columns = vec_ref.shape[1]
    pairs = list(zip(sources, targets))
    pairs.append((sources[0].at[vec_ref.shape[0] - first_ref.shape[0] :, :], first_ref))
    pairs.append((sources[0].at[: second_ref.shape[0], :], second_ref))
    copies = [pltpu.make_async_copy(source, target, sems.at[i]) for i, (source, target) in enumerate(pairs)]
    for copy in copies:
        copy.start()
    for copy in copies:
        copy.wait()
    for leaf in range(leaves):
        coefs_ref[leaf * rank : (leaf + 1) * rank, :] = jnp.dot(
            basis_ref[leaf], vec_ref[leaf * rows : (leaf + 1) * rows, :], preferred_element_type=jnp.float32
        )
    whole = coefs_ref[...]
    transfer = transfer_ref[...].reshape(leaves * rank, rank)
    low = exact(transfer, whole, (0, 0))
    top = exact(cluster_ref[0], low, (0, 0))
    pair_ref[0] = low
    pair_ref[1] = top
    half = (SPARE // 2, columns)
    low, low_power = scale(low)
    top, top_power = scale(top)
    short_ref[:rank, :] = low
    short_ref[rank : 2 * rank, :] = top
    short_ref[2 * rank : 2 * rank + SPARE // 2, :] = jnp.broadcast_to(low_power, half)
    short_ref[2 * rank + SPARE // 2 :, :] = jnp.broadcast_to(top_power, half)
    whole, power = scale(whole)
    length = leaves * rank
    long_ref[:length, :] = whole
    long_ref[length : length + SPARE, :] = jnp.broadcast_to(power, (SPARE, columns))
    long_ref[length + SPARE :, :] = short_ref[...]


def upward(vectors, basis, transfer, cluster_transfer, cluster_coupling, top_coupling):
    leaves, rank, _ = basis.shape
    points, columns = vectors.shape
    f32 = jnp.float32
    arrays = (vectors, basis, transfer, cluster_transfer, cluster_coupling, top_coupling)
    short = 2 * rank + SPARE
    return call(
        upward_body,
        [HBM] * 6,
        [(array.shape, array.dtype) for array in arrays]
        + [
            ((points // 2 + SPARE, columns), vectors.dtype),
            ((points // 2, columns), vectors.dtype),
            ((leaves * rank, columns), f32),
            ((leaves * rank + SPARE + short, columns), f32),
            ((short, columns), f32),
            ((2, rank, columns), f32),
        ],
        scratch=[pltpu.SemaphoreType.DMA((8,))],
        name="leaf_and_cluster_coefs",
    )(*[in_hbm(array) for array in arrays])


def cluster_body(subs, own_ref, low_ref, high_ref, *refs):
    part_refs, (stack_ref, top_ref) = refs[:-2], refs[-2:]
    rank = own_ref.shape[1]
    sub = lax.axis_index("sub")
    tops = [own_ref[1]]

    def put(valid, place, ref):
        at = ref.shape[0] - 2 * rank - SPARE
        values = []
        for i in range(2):
            power = ref[at + 2 * rank + i * SPARE // 2 : at + 2 * rank + i * SPARE // 2 + 1, :]
            values.append(ref[at + i * rank : at + (i + 1) * rank, :] * jnp.exp2(power - 14.0))

        @pl.when(valid)
        def _():
            stack_ref[place] = values[0]

        tops.append(jnp.where(valid, values[1], 0.0))

    stack_ref[sub] = own_ref[0]
    put(sub > 0, sub - 1, low_ref)
    put(sub < subs - 1, sub + 1, high_ref)
    for i, ref in enumerate(part_refs[:-1]):
        put(sub >= 0, lax.rem(sub - 2 - i + subs, subs), ref)
    if part_refs:
        put((sub == 0) | (sub == subs - 1), subs - 1 - sub, part_refs[-1])
    top_ref[0] = functools.reduce(jnp.add, tops)


def cluster_sums(own, low, high, parts):
    _, rank, columns = own.shape
    subs = lax.axis_size("sub")
    return call(
        functools.partial(cluster_body, subs),
        [VMEM] * (3 + len(parts)),
        [((subs, rank, columns), jnp.float32), ((1, rank, columns), jnp.float32)],
        name="sums_over_sub",
    )(own, low, high, *parts)


def join_body(first_ref, second_ref, out_ref):
    width = first_ref.shape[0]
    out_ref[:width] = first_ref[...]
    out_ref[width:] = second_ref[...]


def join(first, second):
    shape = (2 * first.shape[0],) + first.shape[1:]
    return call(join_body, [VMEM] * 2, [(shape, first.dtype)], name="join_cols")(first, second)[0]


def gather_sub(value):
    count = lax.axis_size("sub")
    return [
        lax.ppermute(value, "sub", [(i, (i + step) % count) for i in range(count)])
        for step in range(2, count - 1)
    ]


def onward_body(low_ref, high_ref, out_ref):
    at = low_ref.shape[0] - out_ref.shape[0]
    out_ref[...] = jnp.where(lax.axis_index("sub") == 0, low_ref[at:, :], high_ref[at:, :])


def around(low, high, length):
    subs, cols = lax.axis_size("sub"), lax.axis_size("col")
    onward = call(
        onward_body, [VMEM] * 2, [((length, low.shape[1]), jnp.float32)], name="passed_on"
    )(low, high)[0]
    pairs = []
    for col in range(cols):
        pairs.append((col * subs, (col - 1) % cols * subs))
        pairs.append((col * subs + subs - 1, (col + 1) % cols * subs + subs - 1))
    return lax.ppermute(onward.astype(jnp.float16), BOTH, pairs)


def gather_col(value):
    count = lax.axis_size("col")
    if count & (count - 1):
        return lax.all_gather(value, "col", axis=0, tiled=True)
    width = 1
    while width < count:
        pairs = [(i, i ^ width) for i in range(count)]
        value = join(value, lax.ppermute(value, "col", pairs))
        width *= 2
    return value


def far_body(far_ref, near_ref, coupling_in, low_ref, own_ref, high_ref, field_ref, coupling_ref, window, sems):
    leaves, slots, rank, _ = coupling_ref.shape
    rows = leaves * rank

    def copy(leaf):
        return pltpu.make_async_copy(coupling_in.at[leaf], coupling_ref.at[leaf], sems.at[leaf])

    @pl.loop(0, leaves)
    def _(leaf):
        copy(leaf).start()

    first = near_ref[0, 0] - leaves
    for place, ref in ((0, low_ref), (2, high_ref)):
        scale = jnp.exp2(ref[rows : rows + 1, :] - 14.0)
        window[place * rows : (place + 1) * rows, :] = ref[:rows, :] * scale
    window[rows : 2 * rows, :] = own_ref[...]

    for leaf in range(leaves):
        copy(leaf).wait()
    for leaf in range(leaves):
        picked = []
        for k in range(slots):
            place = jnp.clip(far_ref[k, leaf] - first, 0, 3 * leaves - 1)
            picked.append(window[pl.ds(pl.multiple_of(place * rank, rank), rank), :])
        here = coupling_ref[leaf]
        wide = jnp.concatenate([here[k] for k in range(slots)], axis=1)
        field_ref[leaf * rank : (leaf + 1) * rank, :] = exact(wide, jnp.concatenate(picked, axis=0))


def far(leaf_far, near_index, coupling, low, own, high):
    leaves, _, rank, _ = coupling.shape
    return call(
        far_body,
        [SMEM] * 2 + [HBM] + [VMEM] * 3,
        [(own.shape, jnp.float32)],
        scratch=[
            pltpu.VMEM(coupling.shape, coupling.dtype),
            pltpu.VMEM((3 * leaves * rank, own.shape[1]), jnp.float32),
            pltpu.SemaphoreType.DMA((leaves,)),
        ],
        name="far_field_of_leaves",
    )(leaf_far, near_index, in_hbm(coupling), low, own, high)[0]


def load_body(blocks_ref, held_ref, sem):
    copy = pltpu.make_async_copy(blocks_ref, held_ref, sem)
    copy.start()
    copy.wait()


def load(blocks):
    return pl.pallas_call(
        load_body,
        in_specs=[HBM],
        out_specs=VMEM,
        out_shape=pltpu.VMEM(blocks.shape, blocks.dtype),
        scratch_shapes=[pltpu.SemaphoreType.DMA],
        cost_estimate=pl.CostEstimate(flops=0, bytes_accessed=0, transcendentals=0),
        compiler_params=pltpu.CompilerParams(vmem_limit_bytes=16 * 2**20),
        name="load_near_blocks",
    )(in_hbm(blocks))


def near_body(
    near_ref, blocks_ref, own_ref, high_ref, acc_ref, list_ref, found_ref, window
):
    leaves, slots, rows, _ = blocks_ref.shape

    window[: leaves * rows, :] = own_ref[...]
    window[leaves * rows : 2 * leaves * rows, :] = high_ref[...]
    window[2 * leaves * rows :, :] = jnp.zeros((rows, high_ref.shape[1]), window.dtype)
    first = near_ref[0, 0]

    half = leaves // 2
    room = list_ref.shape[0] // 2
    lane = lax.broadcasted_iota(jnp.int32, (1, list_ref.shape[1]), 1)
    list_ref[...] = jnp.zeros_like(list_ref)

    def note(leaf, carry):
        found, counts = carry
        for k in range(1, slots):
            place = near_ref[k, leaf] - first + leaves
            after = []
            for i, valid in enumerate((place >= half, place < half)):
                valid = valid & (place < leaves)
                at = jnp.maximum(place - (1 - i) * half, 0)
                entry = jnp.where(lane == 0, leaf * slots + k, jnp.where(lane == 1, at, 0))

                @pl.when(valid)
                def _(entry=entry, spot=i * room + counts[i]):
                    list_ref[pl.ds(spot, 1), :] = entry

                one = valid.astype(jnp.int32)
                after.append(counts[i] + one)
                found = found + jnp.where(lane == leaf, one, 0)
            counts = tuple(after)
        return found, counts

    found, counts = lax.fori_loop(
        0, leaves, note, (jnp.zeros(lane.shape, jnp.int32), (jnp.int32(0), jnp.int32(0)))
    )
    found_ref[0:1, :] = found
    found_ref[1:2, :] = jnp.where(lane == 0, counts[0], counts[1])

    for leaf in range(leaves):
        acc = None
        for k in range(slots):
            place = near_ref[k, leaf] - first
            place = jnp.where(place < 0, 2 * leaves, jnp.minimum(place, 2 * leaves - 1))
            start = pl.multiple_of(place * rows, rows)
            term = jnp.dot(
                blocks_ref[leaf, k], window[pl.ds(start, rows), :], preferred_element_type=jnp.float32
            )
            acc = term if acc is None else acc + term
        acc_ref[leaf * rows : (leaf + 1) * rows, :] = acc


def near(near_index, blocks, own, high):
    leaves, slots, rows, _ = blocks.shape
    room = leaves * slots + BATCH
    lanes = -(-max(leaves, 2) // 128) * 128
    return pl.pallas_call(
        near_body,
        in_specs=[SMEM] + [VMEM] * 3,
        out_specs=[VMEM] * 3,
        out_shape=[
            pltpu.VMEM(own.shape, jnp.float32),
            jax.ShapeDtypeStruct((2 * room, lanes), jnp.int32),
            jax.ShapeDtypeStruct((8, lanes), jnp.int32),
        ],
        scratch_shapes=[
            pltpu.VMEM(((2 * leaves + 1) * rows, own.shape[1]), own.dtype),
        ],
        compiler_params=pltpu.CompilerParams(vmem_limit_bytes=32 * 2**20),
        cost_estimate=pl.CostEstimate(flops=0, bytes_accessed=0, transcendentals=0),
        name="near_own_and_high",
    )(near_index, blocks, own, high)


def down_body(
    straight, partner_ref, top_partner_ref, stack_ref, cols_ref, coupling_ref, top_coupling_ref, cluster_ref,
    transfer_ref, field_ref, basis_ref, acc_ref, sum_ref, out_ref, fields, held, sem,
):
    leaves, rank, rows = basis_ref.shape
    col = lax.axis_index("col")
    top = None
    for k in range(top_coupling_ref.shape[1]):
        place = top_partner_ref[0, k]
        place = place if straight else lax.bitwise_xor(place, col)
        term = exact(top_coupling_ref[0, k], cols_ref[place])
        top = term if top is None else top + term
    cluster = exact(cluster_ref[0], top)
    for k in range(coupling_ref.shape[1]):
        cluster = cluster + exact(coupling_ref[0, k], stack_ref[partner_ref[0, k]])
    transfer = transfer_ref[...].reshape(leaves * rank, rank)
    fields[...] = (field_ref[...] + exact(transfer, cluster)).astype(fields.dtype)
    for leaf in range(leaves):
        here = slice(leaf * rows, (leaf + 1) * rows)
        total = acc_ref[here, :] + lax.dot_general(
            basis_ref[leaf],
            fields[leaf * rank : (leaf + 1) * rank, :],
            (((0,), (0,)), ((), ())),
            preferred_element_type=jnp.float32,
        )
        sum_ref[here, :] = total
        held[here, :] = total.astype(held.dtype)
        pltpu.make_async_copy(held.at[here, :], out_ref.at[here, :], sem).start()
    pltpu.make_async_copy(held, out_ref, sem).wait()


def down(partner, top_partner, stack, cols, coupling, top_coupling, cluster_transfer, transfer, field, basis, acc):
    count = lax.axis_size("col")
    return pl.pallas_call(
        functools.partial(down_body, bool(count & (count - 1))),
        in_specs=[SMEM] * 2 + [VMEM] * 9,
        out_specs=[VMEM, HBM],
        out_shape=[jax.ShapeDtypeStruct(acc.shape, jnp.float32), pltpu.HBM(acc.shape, jnp.bfloat16)],
        scratch_shapes=[
            pltpu.VMEM(field.shape, jnp.bfloat16),
            pltpu.VMEM(acc.shape, jnp.bfloat16),
            pltpu.SemaphoreType.DMA,
        ],
        compiler_params=pltpu.CompilerParams(vmem_limit_bytes=16 * 2**20),
        cost_estimate=pl.CostEstimate(flops=0, bytes_accessed=0, transcendentals=0),
        name="fields_down",
    )(partner, top_partner, stack, cols, coupling, top_coupling, cluster_transfer, transfer, field, basis, acc)


def add_listed(list_ref, found_ref, part, batch_size, blocks_ref, low_ref, acc_ref):
    _, slots, rows, _ = blocks_ref.shape
    count = found_ref[1, part]
    room = list_ref.shape[0] // 2

    @pl.loop(0, pl.cdiv(count, batch_size))
    def _(batch):
        terms, ats = [], []
        spots = [part * room + batch * batch_size + i for i in range(batch_size)]
        entries = [(list_ref[spot, 0], list_ref[spot, 1]) for spot in spots]
        for at, place in entries:
            start = pl.multiple_of(place * rows, rows)
            block = blocks_ref[at // slots, lax.rem(at, slots)]
            terms.append(jnp.dot(block, low_ref[pl.ds(start, rows), :], preferred_element_type=jnp.float32))
            ats.append(at)
        for i in range(batch_size):

            @pl.when(batch * batch_size + i < count)
            def _(i=i):
                start = pl.multiple_of(ats[i] // slots * rows, rows)
                acc_ref[pl.ds(start, rows), :] += terms[i]


def low_body(list_ref, found_ref, blocks_ref, low_ref, acc_in, acc_ref):
    add_listed(list_ref, found_ref, 0, BATCH, blocks_ref, low_ref.at[SPARE:, :], acc_ref)


def near_low(places, found, blocks, low, acc):
    return pl.pallas_call(
        low_body,
        in_specs=[VMEM] * 5,
        out_specs=VMEM,
        out_shape=jax.ShapeDtypeStruct(acc.shape, acc.dtype),
        input_output_aliases={4: 0},
        compiler_params=pltpu.CompilerParams(vmem_limit_bytes=16 * 2**20),
        cost_estimate=pl.CostEstimate(flops=0, bytes_accessed=0, transcendentals=0),
        name="near_low_first",
    )(places, found, blocks, low, acc)


def last_body(list_ref, found_ref, blocks_ref, low_ref, acc_ref, out_in, out_ref, held, sems):
    leaves, _, rows, _ = blocks_ref.shape
    touched = [found_ref[0, leaf] for leaf in range(leaves)]
    add_listed(list_ref, found_ref, 1, GROUP, blocks_ref, low_ref, acc_ref)

    def copy(leaf):
        here = slice(leaf * rows, (leaf + 1) * rows)
        return pltpu.make_async_copy(held.at[here, :], out_ref.at[here, :], sems.at[leaf])

    for leaf in range(leaves):

        @pl.when(touched[leaf] > 0)
        def _(leaf=leaf):
            here = slice(leaf * rows, (leaf + 1) * rows)
            held[here, :] = acc_ref[here, :].astype(held.dtype)
            copy(leaf).start()

    for leaf in range(leaves):

        @pl.when(touched[leaf] > 0)
        def _(leaf=leaf):
            copy(leaf).wait()


def last(places, found, blocks, low, acc, out):
    leaves = blocks.shape[0]
    return pl.pallas_call(
        last_body,
        in_specs=[VMEM] * 5 + [HBM],
        out_specs=HBM,
        out_shape=jax.ShapeDtypeStruct(out.shape, out.dtype),
        input_output_aliases={5: 0},
        scratch_shapes=[
            pltpu.VMEM(out.shape, out.dtype),
            pltpu.SemaphoreType.DMA((leaves,)),
        ],
        compiler_params=pltpu.CompilerParams(vmem_limit_bytes=32 * 2**20),
        cost_estimate=pl.CostEstimate(flops=0, bytes_accessed=0, transcendentals=0),
        name="near_low_second",
    )(places, found, blocks, low, acc, out)


def local(
    vectors,
    near_blocks,
    near_index,
    leaf_basis,
    leaf_transfer,
    leaf_coupling,
    leaf_far,
    cluster_transfer,
    cluster_coupling,
    cluster_partner,
    top_coupling,
    top_partner,
):
    high_vec = shift(vectors, -1)
    near_index, leaf_far = near_index.T, leaf_far.T

    own, basis, transfer, cluster, couple, top_couple, first, second, coefs, long, short, pair = upward(
        vectors, leaf_basis, leaf_transfer, cluster_transfer, cluster_coupling, top_coupling
    )
    long, short = long.astype(jnp.float16), short.astype(jnp.float16)
    low_part = shift_around(long, 1)
    high_part = shift_around(long, -1)
    parts = gather_sub(short)
    first, near_blocks, _ = lax.optimization_barrier((first, near_blocks, long))
    blocks = load(near_blocks)
    low_first = shift(first, 1)
    acc, places, found = near(near_index, blocks, own, high_vec)

    second, parts, low_part, high_part, acc = lax.optimization_barrier((second, parts, low_part, high_part, acc))
    low_second = shift(second, 1)

    low_part, high_part = low_part.astype(jnp.float32), high_part.astype(jnp.float32)
    if lax.axis_size("sub") > 2:
        parts = parts + [around(low_part, high_part, short.shape[0])]
    parts = [part.astype(jnp.float32) for part in parts]
    stack, top = cluster_sums(pair, low_part, high_part, parts)
    cols = gather_col(top)
    field = far(leaf_far, near_index, leaf_coupling, low_part, coefs, high_part)
    acc, out = down(
        cluster_partner, top_partner, stack, cols, couple, top_couple, cluster, transfer, field, basis, acc
    )
    acc = near_low(places, found, blocks, low_first, acc)
    return last(places, found, blocks, low_second, acc, out)


def solution(mesh):
    both = P(BOTH)
    in_specs = (both,) * 10 + (P("col"),) * 2
    return jax.shard_map(local, mesh=mesh, in_specs=in_specs, out_specs=both, check_vma=False)
```

```python
import functools

import jax
import jax.numpy as jnp
from jax import lax
from jax.experimental import pallas as pl
from jax.experimental.pallas import tpu as pltpu
from jax.sharding import PartitionSpec as P

HIGHEST = lax.Precision.HIGHEST
BOTH = ("col", "sub")
SPARE = 16
TAIL = 8
GROUP = 4
BATCH = 8
VMEM = pl.BlockSpec(memory_space=pltpu.VMEM)
SMEM = pl.BlockSpec(memory_space=pltpu.SMEM)
HBM = pl.BlockSpec(memory_space=pltpu.HBM)


def call(body, ins, outs, scratch=(), mib=16, name=None):
    return pl.pallas_call(
        body,
        in_specs=ins,
        out_specs=[VMEM] * len(outs),
        out_shape=[jax.ShapeDtypeStruct(shape, kind) for shape, kind in outs],
        scratch_shapes=scratch,
        compiler_params=pltpu.CompilerParams(vmem_limit_bytes=mib * 2**20),
        cost_estimate=pl.CostEstimate(flops=0, bytes_accessed=0, transcendentals=0),
        name=name,
    )


def shift(value, step):
    count = lax.axis_size(BOTH)
    pairs = [(i, i + step) for i in range(count) if 0 <= i + step < count]
    return lax.ppermute(value, BOTH, pairs)


def shift_around(value, by):
    count = lax.axis_size(BOTH)
    return lax.ppermute(value, BOTH, [(i, (i + by) % count) for i in range(count)])


def exact(a, b, contract=(1, 0)):
    dims = (((contract[0],), (contract[1],)), ((), ()))
    return lax.dot_general(a, b, dims, precision=HIGHEST, preferred_element_type=jnp.float32)


def pack(ref, parts):
    at = 0
    row = lax.broadcasted_iota(jnp.int32, (TAIL, ref.shape[1]), 0)
    powers = jnp.zeros(row.shape, jnp.float32)
    for i, part in enumerate(parts):
        most = jnp.max(jnp.abs(part), axis=(0, 1), keepdims=True)
        power = jnp.floor(jnp.log2(jnp.maximum(most, 1e-30)))
        ref[at : at + part.shape[0], :] = part * jnp.exp2(14.0 - power)
        powers = jnp.where(row == i, power, powers)
        at += part.shape[0]
    ref[at:, :] = powers


def unpack(ref, at, length, i):
    row = ref.shape[0] - TAIL + i
    return ref[at : at + length, :] * jnp.exp2(ref[row : row + 1, :] - 14.0)


def in_hbm(value):
    return pltpu.with_memory_space_constraint(value, pltpu.HBM)


def upward_body(*refs):
    sources, targets, refs = refs[:6], refs[6:12], refs[12:]
    vec_ref, basis_ref, transfer_ref, cluster_ref, _, _ = targets
    first_ref, second_ref, coefs_ref, long_ref, short_ref, pair_ref, sems = refs
    leaves, rank, rows = basis_ref.shape
    columns = vec_ref.shape[1]
    pairs = list(zip(sources, targets))
    pairs.append((sources[0].at[vec_ref.shape[0] - first_ref.shape[0] :, :], first_ref))
    pairs.append((sources[0].at[: second_ref.shape[0], :], second_ref))
    copies = [pltpu.make_async_copy(source, target, sems.at[i]) for i, (source, target) in enumerate(pairs)]
    for copy in copies:
        copy.start()
    for copy in copies:
        copy.wait()
    for leaf in range(leaves):
        coefs_ref[leaf * rank : (leaf + 1) * rank, :] = jnp.dot(
            basis_ref[leaf], vec_ref[leaf * rows : (leaf + 1) * rows, :], preferred_element_type=jnp.float32
        )
    whole = coefs_ref[...]
    transfer = transfer_ref[...].reshape(leaves * rank, rank)
    low = exact(transfer, whole, (0, 0))
    top = exact(cluster_ref[0], low, (0, 0))
    pair_ref[0] = low
    pair_ref[1] = top
    matrix = cluster_ref[0]
    height = rank * rank // columns
    wide = jnp.concatenate([matrix[i : i + height, :] for i in range(0, rank, height)], axis=1)
    pack(long_ref, (whole, low, wide))
    short_ref[...] = long_ref[leaves * rank :, :]


def upward(vectors, basis, transfer, cluster_transfer, cluster_coupling, top_coupling):
    leaves, rank, _ = basis.shape
    points, columns = vectors.shape
    f32 = jnp.float32
    arrays = (vectors, basis, transfer, cluster_transfer, cluster_coupling, top_coupling)
    short = rank + rank * rank // columns + TAIL
    return call(
        upward_body,
        [HBM] * 6,
        [(array.shape, array.dtype) for array in arrays]
        + [
            ((points // 2 + SPARE, columns), vectors.dtype),
            ((points // 2, columns), vectors.dtype),
            ((leaves * rank, columns), f32),
            ((leaves * rank + short, columns), f32),
            ((short, columns), f32),
            ((2, rank, columns), f32),
        ],
        scratch=[pltpu.SemaphoreType.DMA((8,))],
        name="leaf_and_cluster_coefs",
    )(*[in_hbm(array) for array in arrays])


def cluster_body(subs, own_ref, low_ref, high_ref, *refs):
    part_refs, (stack_ref, top_ref) = refs[:-2], refs[-2:]
    rank = own_ref.shape[1]
    sub = lax.axis_index("sub")
    matrices, lows = [], []

    columns = own_ref.shape[2]
    height = rank * rank // columns

    def put(valid, place, ref):
        at = ref.shape[0] - rank - height - TAIL
        low = unpack(ref, at, rank, 1)
        wide = unpack(ref, at + rank, height, 2)
        matrix = jnp.concatenate([wide[:, i : i + rank] for i in range(0, columns, rank)], axis=0)

        @pl.when(valid)
        def _():
            stack_ref[place] = low

        matrices.append(matrix)
        lows.append(jnp.where(valid, low, 0.0))

    stack_ref[sub] = own_ref[0]
    put(sub > 0, sub - 1, low_ref)
    put(sub < subs - 1, sub + 1, high_ref)
    for i, ref in enumerate(part_refs[:-1]):
        put(sub >= 0, lax.rem(sub - 2 - i + subs, subs), ref)
    if part_refs:
        put((sub == 0) | (sub == subs - 1), subs - 1 - sub, part_refs[-1])
    top_ref[0] = own_ref[1] + exact(jnp.concatenate(matrices, axis=0), jnp.concatenate(lows, axis=0), (0, 0))


def cluster_sums(own, low, high, parts):
    _, rank, columns = own.shape
    subs = lax.axis_size("sub")
    return call(
        functools.partial(cluster_body, subs),
        [VMEM] * (3 + len(parts)),
        [((subs, rank, columns), jnp.float32), ((1, rank, columns), jnp.float32)],
        name="sums_over_sub",
    )(own, low, high, *parts)


def join_body(first_ref, second_ref, out_ref):
    width = first_ref.shape[0]
    out_ref[:width] = first_ref[...]
    out_ref[width:] = second_ref[...]


def join(first, second):
    shape = (2 * first.shape[0],) + first.shape[1:]
    return call(join_body, [VMEM] * 2, [(shape, first.dtype)], name="join_cols")(first, second)[0]


def gather_sub(value):
    count = lax.axis_size("sub")
    return [
        lax.ppermute(value, "sub", [(i, (i + step) % count) for i in range(count)])
        for step in range(2, count - 1)
    ]


def onward_body(low_ref, high_ref, out_ref):
    at = low_ref.shape[0] - out_ref.shape[0]
    out_ref[...] = jnp.where(lax.axis_index("sub") == 0, low_ref[at:, :], high_ref[at:, :])


def around(low, high, length):
    subs, cols = lax.axis_size("sub"), lax.axis_size("col")
    onward = call(
        onward_body, [VMEM] * 2, [((length, low.shape[1]), jnp.float32)], name="passed_on"
    )(low, high)[0]
    pairs = []
    for col in range(cols):
        pairs.append((col * subs, (col - 1) % cols * subs))
        pairs.append((col * subs + subs - 1, (col + 1) % cols * subs + subs - 1))
    return lax.ppermute(onward.astype(jnp.float16), BOTH, pairs)


def gather_col(value):
    count = lax.axis_size("col")
    if count & (count - 1):
        return lax.all_gather(value, "col", axis=0, tiled=True)
    width = 1
    while width < count:
        pairs = [(i, i ^ width) for i in range(count)]
        value = join(value, lax.ppermute(value, "col", pairs))
        width *= 2
    return value


def split(value):
    head = value.astype(jnp.bfloat16)
    return head, (value - head.astype(jnp.float32)).astype(jnp.bfloat16)


def far_body(far_ref, near_ref, coupling_in, low_ref, own_ref, high_ref, field_ref, coupling_ref, heads, rests, sems):
    leaves, slots, rank, _ = coupling_ref.shape
    rows = leaves * rank

    def copy(leaf):
        return pltpu.make_async_copy(coupling_in.at[leaf], coupling_ref.at[leaf], sems.at[leaf])

    @pl.loop(0, leaves)
    def _(leaf):
        copy(leaf).start()

    first = near_ref[0, 0] - leaves
    for place, ref in ((0, low_ref), (2, high_ref)):
        here = slice(place * rows, (place + 1) * rows)
        heads[here, :], rests[here, :] = split(unpack(ref, 0, rows, 0))
    heads[rows : 2 * rows, :], rests[rows : 2 * rows, :] = split(own_ref[...])

    for leaf in range(leaves):
        copy(leaf).wait()
    for leaf in range(leaves):
        picked = []
        for k in range(slots):
            place = jnp.clip(far_ref[k, leaf] - first, 0, 3 * leaves - 1)
            picked.append(pl.ds(pl.multiple_of(place * rank, rank), rank))
        head = jnp.concatenate([heads[at, :] for at in picked], axis=0)
        rest = jnp.concatenate([rests[at, :] for at in picked], axis=0)
        here = coupling_ref[leaf]
        wide_head, wide_rest = split(jnp.concatenate([here[k] for k in range(slots)], axis=1))
        both = jnp.dot(
            jnp.concatenate([wide_head, wide_rest], axis=0), head, preferred_element_type=jnp.float32
        )
        last = jnp.dot(wide_head, rest, preferred_element_type=jnp.float32)
        field_ref[leaf * rank : (leaf + 1) * rank, :] = both[:rank] + (both[rank:] + last)


def far(leaf_far, near_index, coupling, low, own, high):
    leaves, _, rank, _ = coupling.shape
    return call(
        far_body,
        [SMEM] * 2 + [HBM] + [VMEM] * 3,
        [(own.shape, jnp.float32)],
        scratch=[
            pltpu.VMEM(coupling.shape, coupling.dtype),
            pltpu.VMEM((3 * leaves * rank, own.shape[1]), jnp.bfloat16),
            pltpu.VMEM((3 * leaves * rank, own.shape[1]), jnp.bfloat16),
            pltpu.SemaphoreType.DMA((leaves,)),
        ],
        name="far_field_of_leaves",
    )(leaf_far, near_index, in_hbm(coupling), low, own, high)[0]


def load_body(blocks_ref, held_ref, sem):
    copy = pltpu.make_async_copy(blocks_ref, held_ref, sem)
    copy.start()
    copy.wait()


def load(blocks):
    return pl.pallas_call(
        load_body,
        in_specs=[HBM],
        out_specs=VMEM,
        out_shape=pltpu.VMEM(blocks.shape, blocks.dtype),
        scratch_shapes=[pltpu.SemaphoreType.DMA],
        cost_estimate=pl.CostEstimate(flops=0, bytes_accessed=0, transcendentals=0),
        compiler_params=pltpu.CompilerParams(vmem_limit_bytes=16 * 2**20),
        name="load_near_blocks",
    )(in_hbm(blocks))


def near_body(
    near_ref, blocks_ref, own_ref, high_ref, acc_ref, list_ref, found_ref, window
):
    leaves, slots, rows, _ = blocks_ref.shape

    window[: leaves * rows, :] = own_ref[...]
    window[leaves * rows : 2 * leaves * rows, :] = high_ref[...]
    window[2 * leaves * rows :, :] = jnp.zeros((rows, high_ref.shape[1]), window.dtype)
    first = near_ref[0, 0]

    half = leaves // 2
    room = list_ref.shape[0] // 2
    lane = lax.broadcasted_iota(jnp.int32, (1, list_ref.shape[1]), 1)
    list_ref[...] = jnp.zeros_like(list_ref)

    def note(leaf, carry):
        found, counts = carry
        for k in range(1, slots):
            place = near_ref[k, leaf] - first + leaves
            after = []
            for i, valid in enumerate((place >= half, place < half)):
                valid = valid & (place < leaves)
                at = jnp.maximum(place - (1 - i) * half, 0)
                entry = jnp.where(lane == 0, leaf * slots + k, jnp.where(lane == 1, at, 0))

                @pl.when(valid)
                def _(entry=entry, spot=i * room + counts[i]):
                    list_ref[pl.ds(spot, 1), :] = entry

                one = valid.astype(jnp.int32)
                after.append(counts[i] + one)
            counts = tuple(after)
            found = found + jnp.where((lane == leaf) & (place < half), 1, 0)
        return found, counts

    found, counts = lax.fori_loop(
        0, leaves, note, (jnp.zeros(lane.shape, jnp.int32), (jnp.int32(0), jnp.int32(0)))
    )
    found_ref[0:1, :] = found
    found_ref[1:2, :] = jnp.where(lane == 0, counts[0], counts[1])

    for leaf in range(leaves):
        acc = None
        for k in range(slots):
            place = near_ref[k, leaf] - first
            place = jnp.where(place < 0, 2 * leaves, jnp.minimum(place, 2 * leaves - 1))
            start = pl.multiple_of(place * rows, rows)
            term = jnp.dot(
                blocks_ref[leaf, k], window[pl.ds(start, rows), :], preferred_element_type=jnp.float32
            )
            acc = term if acc is None else acc + term
        acc_ref[leaf * rows : (leaf + 1) * rows, :] = acc


def near(near_index, blocks, own, high):
    leaves, slots, rows, _ = blocks.shape
    room = leaves * slots + BATCH
    lanes = -(-max(leaves, 2) // 128) * 128
    return pl.pallas_call(
        near_body,
        in_specs=[SMEM] + [VMEM] * 3,
        out_specs=[VMEM] * 3,
        out_shape=[
            pltpu.VMEM(own.shape, jnp.float32),
            jax.ShapeDtypeStruct((2 * room, lanes), jnp.int32),
            jax.ShapeDtypeStruct((8, lanes), jnp.int32),
        ],
        scratch_shapes=[
            pltpu.VMEM(((2 * leaves + 1) * rows, own.shape[1]), own.dtype),
        ],
        compiler_params=pltpu.CompilerParams(vmem_limit_bytes=32 * 2**20),
        cost_estimate=pl.CostEstimate(flops=0, bytes_accessed=0, transcendentals=0),
        name="near_own_and_high",
    )(near_index, blocks, own, high)


def down_body(
    straight, partner_ref, top_partner_ref, stack_ref, cols_ref, coupling_ref, top_coupling_ref, cluster_ref,
    transfer_ref, field_ref, basis_ref, acc_ref, sum_ref, fields,
):
    leaves, rank, rows = basis_ref.shape
    col = lax.axis_index("col")
    slots = top_coupling_ref.shape[1]
    picked = []
    for k in range(slots):
        place = top_partner_ref[0, k]
        picked.append(cols_ref[place if straight else lax.bitwise_xor(place, col)])
    wide = jnp.concatenate([top_coupling_ref[0, k] for k in range(slots)], axis=1)
    top = exact(wide, jnp.concatenate(picked, axis=0))
    slots = coupling_ref.shape[1]
    picked = [stack_ref[partner_ref[0, k]] for k in range(slots)] + [top]
    wide = jnp.concatenate([coupling_ref[0, k] for k in range(slots)] + [cluster_ref[0]], axis=1)
    cluster = exact(wide, jnp.concatenate(picked, axis=0))
    transfer = transfer_ref[...].reshape(leaves * rank, rank)
    fields[...] = (field_ref[...] + exact(transfer, cluster)).astype(fields.dtype)
    for leaf in range(leaves):
        here = slice(leaf * rows, (leaf + 1) * rows)
        sum_ref[here, :] = acc_ref[here, :] + lax.dot_general(
            basis_ref[leaf],
            fields[leaf * rank : (leaf + 1) * rank, :],
            (((0,), (0,)), ((), ())),
            preferred_element_type=jnp.float32,
        )


def down(partner, top_partner, stack, cols, coupling, top_coupling, cluster_transfer, transfer, field, basis, acc):
    count = lax.axis_size("col")
    return pl.pallas_call(
        functools.partial(down_body, bool(count & (count - 1))),
        in_specs=[SMEM] * 2 + [VMEM] * 9,
        out_specs=VMEM,
        out_shape=pltpu.VMEM(acc.shape, jnp.float32),
        scratch_shapes=[pltpu.VMEM(field.shape, jnp.bfloat16)],
        compiler_params=pltpu.CompilerParams(vmem_limit_bytes=16 * 2**20),
        cost_estimate=pl.CostEstimate(flops=0, bytes_accessed=0, transcendentals=0),
        name="fields_down",
    )(partner, top_partner, stack, cols, coupling, top_coupling, cluster_transfer, transfer, field, basis, acc)


def add_listed(list_ref, found_ref, part, batch_size, blocks_ref, low_ref, acc_ref):
    _, slots, rows, _ = blocks_ref.shape
    count = found_ref[1, part]
    room = list_ref.shape[0] // 2

    @pl.loop(0, pl.cdiv(count, batch_size))
    def _(batch):
        terms, ats = [], []
        spots = [part * room + batch * batch_size + i for i in range(batch_size)]
        entries = [(list_ref[spot, 0], list_ref[spot, 1]) for spot in spots]
        for at, place in entries:
            start = pl.multiple_of(place * rows, rows)
            block = blocks_ref[at // slots, lax.rem(at, slots)]
            terms.append(jnp.dot(block, low_ref[pl.ds(start, rows), :], preferred_element_type=jnp.float32))
            ats.append(at)
        for i in range(batch_size):

            @pl.when(batch * batch_size + i < count)
            def _(i=i):
                start = pl.multiple_of(ats[i] // slots * rows, rows)
                acc_ref[pl.ds(start, rows), :] += terms[i]


def write(leaves, chosen, acc_ref, out_ref, held, sems):
    rows = acc_ref.shape[0] // leaves

    def copy(leaf):
        here = slice(leaf * rows, (leaf + 1) * rows)
        return pltpu.make_async_copy(held.at[here, :], out_ref.at[here, :], sems.at[leaf])

    for leaf in range(leaves):

        @pl.when(chosen[leaf])
        def _(leaf=leaf):
            here = slice(leaf * rows, (leaf + 1) * rows)
            held[here, :] = acc_ref[here, :].astype(held.dtype)
            copy(leaf).start()

    for leaf in range(leaves):

        @pl.when(chosen[leaf])
        def _(leaf=leaf):
            copy(leaf).wait()


def first_body(list_ref, found_ref, blocks_ref, low_ref, acc_in, acc_ref, out_ref, held, sems):
    leaves = blocks_ref.shape[0]
    final = [found_ref[0, leaf] == 0 for leaf in range(leaves)]
    add_listed(list_ref, found_ref, 0, BATCH, blocks_ref, low_ref.at[SPARE:, :], acc_ref)
    write(leaves, final, acc_ref, out_ref, held, sems)


def near_low(places, found, blocks, low, acc):
    leaves = blocks.shape[0]
    return pl.pallas_call(
        first_body,
        in_specs=[VMEM] * 5,
        out_specs=[VMEM, HBM],
        out_shape=[pltpu.VMEM(acc.shape, acc.dtype), pltpu.HBM(acc.shape, low.dtype)],
        input_output_aliases={4: 0},
        scratch_shapes=[
            pltpu.VMEM(acc.shape, low.dtype),
            pltpu.SemaphoreType.DMA((leaves,)),
        ],
        compiler_params=pltpu.CompilerParams(vmem_limit_bytes=16 * 2**20),
        cost_estimate=pl.CostEstimate(flops=0, bytes_accessed=0, transcendentals=0),
        name="near_low_first",
    )(places, found, blocks, low, acc)


def last_body(list_ref, found_ref, blocks_ref, low_ref, acc_ref, out_in, out_ref, held, sems):
    leaves = blocks_ref.shape[0]
    touched = [found_ref[0, leaf] > 0 for leaf in range(leaves)]
    add_listed(list_ref, found_ref, 1, GROUP, blocks_ref, low_ref, acc_ref)
    write(leaves, touched, acc_ref, out_ref, held, sems)


def last(places, found, blocks, low, acc, out):
    leaves = blocks.shape[0]
    return pl.pallas_call(
        last_body,
        in_specs=[VMEM] * 5 + [HBM],
        out_specs=HBM,
        out_shape=jax.ShapeDtypeStruct(out.shape, out.dtype),
        input_output_aliases={5: 0},
        scratch_shapes=[
            pltpu.VMEM(out.shape, out.dtype),
            pltpu.SemaphoreType.DMA((leaves,)),
        ],
        compiler_params=pltpu.CompilerParams(vmem_limit_bytes=16 * 2**20),
        cost_estimate=pl.CostEstimate(flops=0, bytes_accessed=0, transcendentals=0),
        name="near_low_second",
    )(places, found, blocks, low, acc, out)


def local(
    vectors,
    near_blocks,
    near_index,
    leaf_basis,
    leaf_transfer,
    leaf_coupling,
    leaf_far,
    cluster_transfer,
    cluster_coupling,
    cluster_partner,
    top_coupling,
    top_partner,
):
    high_vec = shift(vectors, -1)
    near_index, leaf_far = near_index.T, leaf_far.T

    own, basis, transfer, cluster, couple, top_couple, first, second, coefs, long, short, pair = upward(
        vectors, leaf_basis, leaf_transfer, cluster_transfer, cluster_coupling, top_coupling
    )
    long, short = long.astype(jnp.float16), short.astype(jnp.float16)
    low_part = shift_around(long, 1)
    high_part = shift_around(long, -1)
    parts = gather_sub(short)
    first, near_blocks, _ = lax.optimization_barrier((first, near_blocks, long))
    blocks = load(near_blocks)
    low_first = shift(first, 1)
    acc, places, found = near(near_index, blocks, own, high_vec)

    second, parts, low_part, high_part, acc = lax.optimization_barrier((second, parts, low_part, high_part, acc))
    low_second = shift(second, 1)

    low_part, high_part = low_part.astype(jnp.float32), high_part.astype(jnp.float32)
    if lax.axis_size("sub") > 2:
        parts = parts + [around(low_part, high_part, short.shape[0])]
    parts = [part.astype(jnp.float32) for part in parts]
    stack, top = cluster_sums(pair, low_part, high_part, parts)
    cols = gather_col(top)
    field = far(leaf_far, near_index, leaf_coupling, low_part, coefs, high_part)
    acc = down(
        cluster_partner, top_partner, stack, cols, couple, top_couple, cluster, transfer, field, basis, acc
    )
    acc, out = near_low(places, found, blocks, low_first, acc)
    return last(places, found, blocks, low_second, acc, out)


def solution(mesh):
    both = P(BOTH)
    in_specs = (both,) * 10 + (P("col"),) * 2
    return jax.shard_map(local, mesh=mesh, in_specs=in_specs, out_specs=both, check_vma=False)
```

```python
import functools

import jax
import jax.numpy as jnp
from jax import lax
from jax.experimental import pallas as pl
from jax.experimental.pallas import tpu as pltpu
from jax.sharding import PartitionSpec as P

HIGHEST = lax.Precision.HIGHEST
BOTH = ("col", "sub")
SPARE = 16
TAIL = 8
GROUP = 4
BATCH = 8
VMEM = pl.BlockSpec(memory_space=pltpu.VMEM)
SMEM = pl.BlockSpec(memory_space=pltpu.SMEM)
HBM = pl.BlockSpec(memory_space=pltpu.HBM)


def call(body, ins, outs, scratch=(), mib=16, name=None):
    return pl.pallas_call(
        body,
        in_specs=ins,
        out_specs=[VMEM] * len(outs),
        out_shape=[jax.ShapeDtypeStruct(shape, kind) for shape, kind in outs],
        scratch_shapes=scratch,
        compiler_params=pltpu.CompilerParams(vmem_limit_bytes=mib * 2**20),
        cost_estimate=pl.CostEstimate(flops=0, bytes_accessed=0, transcendentals=0),
        name=name,
    )


def shift(value, step):
    count = lax.axis_size(BOTH)
    pairs = [(i, i + step) for i in range(count) if 0 <= i + step < count]
    return lax.ppermute(value, BOTH, pairs)


def shift_around(value, by):
    count = lax.axis_size(BOTH)
    return lax.ppermute(value, BOTH, [(i, (i + by) % count) for i in range(count)])


def exact(a, b, contract=(1, 0)):
    dims = (((contract[0],), (contract[1],)), ((), ()))
    return lax.dot_general(a, b, dims, precision=HIGHEST, preferred_element_type=jnp.float32)


def pack(ref, parts):
    at = 0
    row = lax.broadcasted_iota(jnp.int32, (TAIL, ref.shape[1]), 0)
    powers = jnp.zeros(row.shape, jnp.float32)
    for i, part in enumerate(parts):
        most = jnp.max(jnp.abs(part), axis=(0, 1), keepdims=True)
        power = jnp.floor(jnp.log2(jnp.maximum(most, 1e-30)))
        ref[at : at + part.shape[0], :] = part * jnp.exp2(14.0 - power)
        powers = jnp.where(row == i, power, powers)
        at += part.shape[0]
    ref[at:, :] = powers


def unpack(ref, at, length, i):
    row = ref.shape[0] - TAIL + i
    return ref[at : at + length, :] * jnp.exp2(ref[row : row + 1, :] - 14.0)


def in_hbm(value):
    return pltpu.with_memory_space_constraint(value, pltpu.HBM)


def upward_body(*refs):
    sources, targets, refs = refs[:6], refs[6:12], refs[12:]
    vec_ref, basis_ref, transfer_ref, cluster_ref, _, _ = targets
    first_ref, second_ref, coefs_ref, long_ref, short_ref, pair_ref, sems = refs
    leaves, rank, rows = basis_ref.shape
    columns = vec_ref.shape[1]
    pairs = list(zip(sources, targets))
    pairs.append((sources[0].at[vec_ref.shape[0] - first_ref.shape[0] :, :], first_ref))
    pairs.append((sources[0].at[: second_ref.shape[0], :], second_ref))
    copies = [pltpu.make_async_copy(source, target, sems.at[i]) for i, (source, target) in enumerate(pairs)]
    for copy in copies:
        copy.start()
    for copy in copies:
        copy.wait()
    for leaf in range(leaves):
        coefs_ref[leaf * rank : (leaf + 1) * rank, :] = jnp.dot(
            basis_ref[leaf], vec_ref[leaf * rows : (leaf + 1) * rows, :], preferred_element_type=jnp.float32
        )
    whole = coefs_ref[...]
    transfer = transfer_ref[...].reshape(leaves * rank, rank)
    low = exact(transfer, whole, (0, 0))
    top = exact(cluster_ref[0], low, (0, 0))
    pair_ref[0] = low
    pair_ref[1] = top
    matrix = cluster_ref[0]
    height = rank * rank // columns
    wide = jnp.concatenate([matrix[i : i + height, :] for i in range(0, rank, height)], axis=1)
    pack(long_ref, (whole, low, wide))
    short_ref[...] = long_ref[leaves * rank :, :]


def upward(vectors, basis, transfer, cluster_transfer, cluster_coupling, top_coupling):
    leaves, rank, _ = basis.shape
    points, columns = vectors.shape
    f32 = jnp.float32
    arrays = (vectors, basis, transfer, cluster_transfer, cluster_coupling, top_coupling)
    short = rank + rank * rank // columns + TAIL
    return call(
        upward_body,
        [HBM] * 6,
        [(array.shape, array.dtype) for array in arrays]
        + [
            ((points // 2 + SPARE, columns), vectors.dtype),
            ((points // 2, columns), vectors.dtype),
            ((leaves * rank, columns), f32),
            ((leaves * rank + short, columns), f32),
            ((short, columns), f32),
            ((2, rank, columns), f32),
        ],
        scratch=[pltpu.SemaphoreType.DMA((8,))],
        name="leaf_and_cluster_coefs",
    )(*[in_hbm(array) for array in arrays])


def cluster_body(subs, own_ref, low_ref, high_ref, *refs):
    part_refs, (stack_ref, top_ref) = refs[:-2], refs[-2:]
    rank = own_ref.shape[1]
    sub = lax.axis_index("sub")
    matrices, lows = [], []

    columns = own_ref.shape[2]
    height = rank * rank // columns

    def put(valid, place, ref):
        at = ref.shape[0] - rank - height - TAIL
        low = unpack(ref, at, rank, 1)
        wide = unpack(ref, at + rank, height, 2)
        matrix = jnp.concatenate([wide[:, i : i + rank] for i in range(0, columns, rank)], axis=0)

        @pl.when(valid)
        def _():
            stack_ref[place] = low

        matrices.append(matrix)
        lows.append(jnp.where(valid, low, 0.0))

    stack_ref[sub] = own_ref[0]
    put(sub > 0, sub - 1, low_ref)
    put(sub < subs - 1, sub + 1, high_ref)
    for i, ref in enumerate(part_refs[:-1]):
        put(sub >= 0, lax.rem(sub - 2 - i + subs, subs), ref)
    if part_refs:
        put((sub == 0) | (sub == subs - 1), subs - 1 - sub, part_refs[-1])
    top_ref[0] = own_ref[1] + exact(jnp.concatenate(matrices, axis=0), jnp.concatenate(lows, axis=0), (0, 0))


def cluster_sums(own, low, high, parts):
    _, rank, columns = own.shape
    subs = lax.axis_size("sub")
    return call(
        functools.partial(cluster_body, subs),
        [VMEM] * (3 + len(parts)),
        [((subs, rank, columns), jnp.float32), ((1, rank, columns), jnp.float32)],
        name="sums_over_sub",
    )(own, low, high, *parts)


def join_body(first_ref, second_ref, out_ref):
    width = first_ref.shape[0]
    out_ref[:width] = first_ref[...]
    out_ref[width:] = second_ref[...]


def join(first, second):
    shape = (2 * first.shape[0],) + first.shape[1:]
    return call(join_body, [VMEM] * 2, [(shape, first.dtype)], name="join_cols")(first, second)[0]


def gather_sub(value):
    count = lax.axis_size("sub")
    return [
        lax.ppermute(value, "sub", [(i, (i + step) % count) for i in range(count)])
        for step in range(2, count - 1)
    ]


def onward_body(low_ref, high_ref, out_ref):
    at = low_ref.shape[0] - out_ref.shape[0]
    out_ref[...] = jnp.where(lax.axis_index("sub") == 0, low_ref[at:, :], high_ref[at:, :])


def around(low, high, length):
    subs, cols = lax.axis_size("sub"), lax.axis_size("col")
    onward = call(
        onward_body, [VMEM] * 2, [((length, low.shape[1]), jnp.float32)], name="passed_on"
    )(low, high)[0]
    pairs = []
    for col in range(cols):
        pairs.append((col * subs, (col - 1) % cols * subs))
        pairs.append((col * subs + subs - 1, (col + 1) % cols * subs + subs - 1))
    return lax.ppermute(onward.astype(jnp.float16), BOTH, pairs)


def gather_col(value):
    count = lax.axis_size("col")
    if count & (count - 1):
        return lax.all_gather(value, "col", axis=0, tiled=True)
    width = 1
    while width < count:
        pairs = [(i, i ^ width) for i in range(count)]
        value = join(value, lax.ppermute(value, "col", pairs))
        width *= 2
    return value


def split(value):
    head = value.astype(jnp.bfloat16)
    return head, (value - head.astype(jnp.float32)).astype(jnp.bfloat16)


def far_body(far_ref, near_ref, coupling_in, low_ref, own_ref, high_ref, field_ref, coupling_ref, heads, rests, sems):
    leaves, slots, rank, _ = coupling_ref.shape
    rows = leaves * rank

    def copy(leaf):
        return pltpu.make_async_copy(coupling_in.at[leaf], coupling_ref.at[leaf], sems.at[leaf])

    @pl.loop(0, leaves)
    def _(leaf):
        copy(leaf).start()

    first = near_ref[0, 0] - leaves
    for place, ref in ((0, low_ref), (2, high_ref)):
        here = slice(place * rows, (place + 1) * rows)
        heads[here, :], rests[here, :] = split(unpack(ref, 0, rows, 0))
    heads[rows : 2 * rows, :], rests[rows : 2 * rows, :] = split(own_ref[...])

    for leaf in range(leaves):
        copy(leaf).wait()
    for leaf in range(leaves):
        picked = []
        for k in range(slots):
            place = jnp.clip(far_ref[k, leaf] - first, 0, 3 * leaves - 1)
            picked.append(pl.ds(pl.multiple_of(place * rank, rank), rank))
        head = jnp.concatenate([heads[at, :] for at in picked], axis=0)
        rest = jnp.concatenate([rests[at, :] for at in picked], axis=0)
        here = coupling_ref[leaf]
        wide_head, wide_rest = split(jnp.concatenate([here[k] for k in range(slots)], axis=1))
        both = jnp.dot(
            jnp.concatenate([wide_head, wide_rest], axis=0), head, preferred_element_type=jnp.float32
        )
        last = jnp.dot(wide_head, rest, preferred_element_type=jnp.float32)
        field_ref[leaf * rank : (leaf + 1) * rank, :] = both[:rank] + (both[rank:] + last)


def far(leaf_far, near_index, coupling, low, own, high):
    leaves, _, rank, _ = coupling.shape
    return call(
        far_body,
        [SMEM] * 2 + [HBM] + [VMEM] * 3,
        [(own.shape, jnp.float32)],
        scratch=[
            pltpu.VMEM(coupling.shape, coupling.dtype),
            pltpu.VMEM((3 * leaves * rank, own.shape[1]), jnp.bfloat16),
            pltpu.VMEM((3 * leaves * rank, own.shape[1]), jnp.bfloat16),
            pltpu.SemaphoreType.DMA((leaves,)),
        ],
        name="far_field_of_leaves",
    )(leaf_far, near_index, in_hbm(coupling), low, own, high)[0]


def load_body(blocks_ref, held_ref, sem):
    copy = pltpu.make_async_copy(blocks_ref, held_ref, sem)
    copy.start()
    copy.wait()


def load(blocks):
    return pl.pallas_call(
        load_body,
        in_specs=[HBM],
        out_specs=VMEM,
        out_shape=pltpu.VMEM(blocks.shape, blocks.dtype),
        scratch_shapes=[pltpu.SemaphoreType.DMA],
        cost_estimate=pl.CostEstimate(flops=0, bytes_accessed=0, transcendentals=0),
        compiler_params=pltpu.CompilerParams(vmem_limit_bytes=16 * 2**20),
        name="load_near_blocks",
    )(in_hbm(blocks))


def near_body(
    near_ref, blocks_ref, own_ref, high_ref, acc_ref, list_ref, found_ref, window
):
    leaves, slots, rows, _ = blocks_ref.shape

    window[: leaves * rows, :] = own_ref[...]
    window[leaves * rows : 2 * leaves * rows, :] = high_ref[...]
    window[2 * leaves * rows :, :] = jnp.zeros((rows, high_ref.shape[1]), window.dtype)
    first = near_ref[0, 0]

    half = leaves // 2
    room = list_ref.shape[0] // 2
    lane = lax.broadcasted_iota(jnp.int32, (1, list_ref.shape[1]), 1)
    list_ref[...] = jnp.zeros_like(list_ref)

    def note(leaf, carry):
        mask, counts = carry
        for k in range(1, slots):
            place = near_ref[k, leaf] - first + leaves
            after = []
            for i, valid in enumerate((place >= half, place < half)):
                valid = valid & (place < leaves)
                at = jnp.maximum(place - (1 - i) * half, 0)
                entry = jnp.where(lane == 0, leaf * slots + k, jnp.where(lane == 1, at, 0))

                @pl.when(valid)
                def _(entry=entry, spot=i * room + counts[i]):
                    list_ref[pl.ds(spot, 1), :] = entry

                one = valid.astype(jnp.int32)
                after.append(counts[i] + one)
            counts = tuple(after)
            mask = mask | jnp.where(place < half, lax.shift_left(jnp.int32(1), leaf), 0)
        return mask, counts

    zero = jnp.int32(0)
    mask, counts = lax.fori_loop(0, leaves, note, (zero, (zero, zero)))
    found_ref[0:1, :] = jnp.broadcast_to(mask, lane.shape)
    found_ref[1:2, :] = jnp.where(lane == 0, counts[0], counts[1])

    for leaf in range(leaves):
        acc = None
        for k in range(slots):
            place = near_ref[k, leaf] - first
            place = jnp.where(place < 0, 2 * leaves, jnp.minimum(place, 2 * leaves - 1))
            start = pl.multiple_of(place * rows, rows)
            term = jnp.dot(
                blocks_ref[leaf, k], window[pl.ds(start, rows), :], preferred_element_type=jnp.float32
            )
            acc = term if acc is None else acc + term
        acc_ref[leaf * rows : (leaf + 1) * rows, :] = acc


def near(near_index, blocks, own, high):
    leaves, slots, rows, _ = blocks.shape
    room = leaves * slots + 2 * BATCH
    lanes = -(-max(leaves, 2) // 128) * 128
    return pl.pallas_call(
        near_body,
        in_specs=[SMEM] + [VMEM] * 3,
        out_specs=[VMEM] * 3,
        out_shape=[
            pltpu.VMEM(own.shape, jnp.float32),
            jax.ShapeDtypeStruct((2 * room, lanes), jnp.int32),
            jax.ShapeDtypeStruct((8, lanes), jnp.int32),
        ],
        scratch_shapes=[
            pltpu.VMEM(((2 * leaves + 1) * rows, own.shape[1]), own.dtype),
        ],
        compiler_params=pltpu.CompilerParams(vmem_limit_bytes=32 * 2**20),
        cost_estimate=pl.CostEstimate(flops=0, bytes_accessed=0, transcendentals=0),
        name="near_own_and_high",
    )(near_index, blocks, own, high)


def down_body(
    straight, partner_ref, top_partner_ref, stack_ref, cols_ref, coupling_ref, top_coupling_ref, cluster_ref,
    transfer_ref, field_ref, basis_ref, acc_ref, sum_ref, fields,
):
    leaves, rank, rows = basis_ref.shape
    col = lax.axis_index("col")
    slots = top_coupling_ref.shape[1]
    picked = []
    for k in range(slots):
        place = top_partner_ref[0, k]
        picked.append(cols_ref[place if straight else lax.bitwise_xor(place, col)])
    wide = jnp.concatenate([top_coupling_ref[0, k] for k in range(slots)], axis=1)
    top = exact(wide, jnp.concatenate(picked, axis=0))
    slots = coupling_ref.shape[1]
    picked = [stack_ref[partner_ref[0, k]] for k in range(slots)] + [top]
    wide = jnp.concatenate([coupling_ref[0, k] for k in range(slots)] + [cluster_ref[0]], axis=1)
    cluster = exact(wide, jnp.concatenate(picked, axis=0))
    transfer = transfer_ref[...].reshape(leaves * rank, rank)
    fields[...] = (field_ref[...] + exact(transfer, cluster)).astype(fields.dtype)
    for leaf in range(leaves):
        here = slice(leaf * rows, (leaf + 1) * rows)
        sum_ref[here, :] = acc_ref[here, :] + lax.dot_general(
            basis_ref[leaf],
            fields[leaf * rank : (leaf + 1) * rank, :],
            (((0,), (0,)), ((), ())),
            preferred_element_type=jnp.float32,
        )


def down(partner, top_partner, stack, cols, coupling, top_coupling, cluster_transfer, transfer, field, basis, acc):
    count = lax.axis_size("col")
    return pl.pallas_call(
        functools.partial(down_body, bool(count & (count - 1))),
        in_specs=[SMEM] * 2 + [VMEM] * 9,
        out_specs=VMEM,
        out_shape=pltpu.VMEM(acc.shape, jnp.float32),
        scratch_shapes=[pltpu.VMEM(field.shape, jnp.bfloat16)],
        compiler_params=pltpu.CompilerParams(vmem_limit_bytes=16 * 2**20),
        cost_estimate=pl.CostEstimate(flops=0, bytes_accessed=0, transcendentals=0),
        name="fields_down",
    )(partner, top_partner, stack, cols, coupling, top_coupling, cluster_transfer, transfer, field, basis, acc)


def add_listed(list_ref, found_ref, part, batch_size, blocks_ref, low_ref, acc_ref):
    _, slots, rows, _ = blocks_ref.shape
    count = found_ref[1, part]
    room = list_ref.shape[0] // 2

    def read(batch):
        spots = [part * room + batch * batch_size + i for i in range(batch_size)]
        return [(list_ref[spot, 0], list_ref[spot, 1]) for spot in spots]

    def add(batch, entries):
        coming = read(batch + 1)
        terms = []
        for at, place in entries:
            start = pl.multiple_of(place * rows, rows)
            block = blocks_ref[at // slots, lax.rem(at, slots)]
            terms.append(jnp.dot(block, low_ref[pl.ds(start, rows), :], preferred_element_type=jnp.float32))
        for i, (at, _) in enumerate(entries):
            start = pl.multiple_of(at // slots * rows, rows)
            term = jnp.where(batch * batch_size + i < count, terms[i], 0.0)
            acc_ref[pl.ds(start, rows), :] += term
        return coming

    lax.fori_loop(0, pl.cdiv(count, batch_size), add, read(0))


def write(leaves, chosen, acc_ref, out_ref, held, sems):
    rows = acc_ref.shape[0] // leaves

    def copy(leaf):
        here = slice(leaf * rows, (leaf + 1) * rows)
        return pltpu.make_async_copy(held.at[here, :], out_ref.at[here, :], sems.at[leaf])

    for leaf in range(leaves):

        @pl.when(chosen[leaf])
        def _(leaf=leaf):
            here = slice(leaf * rows, (leaf + 1) * rows)
            held[here, :] = acc_ref[here, :].astype(held.dtype)
            copy(leaf).start()

    for leaf in range(leaves):

        @pl.when(chosen[leaf])
        def _(leaf=leaf):
            copy(leaf).wait()


def first_body(list_ref, found_ref, blocks_ref, low_ref, acc_in, acc_ref, out_ref, held, sems):
    leaves = blocks_ref.shape[0]
    mask = found_ref[0, 0]
    final = [mask & (1 << leaf) == 0 for leaf in range(leaves)]
    add_listed(list_ref, found_ref, 0, BATCH, blocks_ref, low_ref.at[SPARE:, :], acc_ref)
    write(leaves, final, acc_ref, out_ref, held, sems)


def near_low(places, found, blocks, low, acc):
    leaves = blocks.shape[0]
    return pl.pallas_call(
        first_body,
        in_specs=[VMEM] * 5,
        out_specs=[VMEM, HBM],
        out_shape=[pltpu.VMEM(acc.shape, acc.dtype), pltpu.HBM(acc.shape, low.dtype)],
        input_output_aliases={4: 0},
        scratch_shapes=[
            pltpu.VMEM(acc.shape, low.dtype),
            pltpu.SemaphoreType.DMA((leaves,)),
        ],
        compiler_params=pltpu.CompilerParams(vmem_limit_bytes=16 * 2**20),
        cost_estimate=pl.CostEstimate(flops=0, bytes_accessed=0, transcendentals=0),
        name="near_low_first",
    )(places, found, blocks, low, acc)


def last_body(list_ref, found_ref, blocks_ref, low_ref, acc_ref, out_in, out_ref, held, sems):
    leaves = blocks_ref.shape[0]
    mask = found_ref[0, 0]
    touched = [mask & (1 << leaf) != 0 for leaf in range(leaves)]
    add_listed(list_ref, found_ref, 1, GROUP, blocks_ref, low_ref, acc_ref)
    write(leaves, touched, acc_ref, out_ref, held, sems)


def last(places, found, blocks, low, acc, out):
    leaves = blocks.shape[0]
    return pl.pallas_call(
        last_body,
        in_specs=[VMEM] * 5 + [HBM],
        out_specs=HBM,
        out_shape=jax.ShapeDtypeStruct(out.shape, out.dtype),
        input_output_aliases={5: 0},
        scratch_shapes=[
            pltpu.VMEM(out.shape, out.dtype),
            pltpu.SemaphoreType.DMA((leaves,)),
        ],
        compiler_params=pltpu.CompilerParams(vmem_limit_bytes=16 * 2**20),
        cost_estimate=pl.CostEstimate(flops=0, bytes_accessed=0, transcendentals=0),
        name="near_low_second",
    )(places, found, blocks, low, acc, out)


def local(
    vectors,
    near_blocks,
    near_index,
    leaf_basis,
    leaf_transfer,
    leaf_coupling,
    leaf_far,
    cluster_transfer,
    cluster_coupling,
    cluster_partner,
    top_coupling,
    top_partner,
):
    high_vec = shift(vectors, -1)
    near_index, leaf_far = near_index.T, leaf_far.T

    own, basis, transfer, cluster, couple, top_couple, first, second, coefs, long, short, pair = upward(
        vectors, leaf_basis, leaf_transfer, cluster_transfer, cluster_coupling, top_coupling
    )
    long, short = long.astype(jnp.float16), short.astype(jnp.float16)
    low_part = shift_around(long, 1)
    high_part = shift_around(long, -1)
    parts = gather_sub(short)
    first, near_blocks, _ = lax.optimization_barrier((first, near_blocks, long))
    blocks = load(near_blocks)
    low_first = shift(first, 1)
    acc, places, found = near(near_index, blocks, own, high_vec)

    second, parts, low_part, high_part, acc = lax.optimization_barrier((second, parts, low_part, high_part, acc))
    low_second = shift(second, 1)

    low_part, high_part = low_part.astype(jnp.float32), high_part.astype(jnp.float32)
    if lax.axis_size("sub") > 2:
        parts = parts + [around(low_part, high_part, short.shape[0])]
    parts = [part.astype(jnp.float32) for part in parts]
    stack, top = cluster_sums(pair, low_part, high_part, parts)
    cols = gather_col(top)
    field = far(leaf_far, near_index, leaf_coupling, low_part, coefs, high_part)
    acc = down(
        cluster_partner, top_partner, stack, cols, couple, top_couple, cluster, transfer, field, basis, acc
    )
    acc, out = near_low(places, found, blocks, low_first, acc)
    return last(places, found, blocks, low_second, acc, out)


def solution(mesh):
    both = P(BOTH)
    in_specs = (both,) * 10 + (P("col"),) * 2
    return jax.shard_map(local, mesh=mesh, in_specs=in_specs, out_specs=both, check_vma=False)
```

```python
import functools

import jax
import jax.numpy as jnp
from jax import lax
from jax.experimental import pallas as pl
from jax.experimental.pallas import tpu as pltpu
from jax.sharding import PartitionSpec as P

HIGHEST = lax.Precision.HIGHEST
BOTH = ("col", "sub")
SPARE = 16
TAIL = 8
GROUP = 4
BATCH = 8
VMEM = pl.BlockSpec(memory_space=pltpu.VMEM)
SMEM = pl.BlockSpec(memory_space=pltpu.SMEM)
HBM = pl.BlockSpec(memory_space=pltpu.HBM)


def call(body, ins, outs, scratch=(), mib=16, name=None):
    return pl.pallas_call(
        body,
        in_specs=ins,
        out_specs=[VMEM] * len(outs),
        out_shape=[jax.ShapeDtypeStruct(shape, kind) for shape, kind in outs],
        scratch_shapes=scratch,
        compiler_params=pltpu.CompilerParams(vmem_limit_bytes=mib * 2**20),
        cost_estimate=pl.CostEstimate(flops=0, bytes_accessed=0, transcendentals=0),
        name=name,
    )


def shift(value, step):
    count = lax.axis_size(BOTH)
    pairs = [(i, i + step) for i in range(count) if 0 <= i + step < count]
    return lax.ppermute(value, BOTH, pairs)


def shift_around(value, by):
    count = lax.axis_size(BOTH)
    return lax.ppermute(value, BOTH, [(i, (i + by) % count) for i in range(count)])


def exact(a, b, contract=(1, 0)):
    dims = (((contract[0],), (contract[1],)), ((), ()))
    return lax.dot_general(a, b, dims, precision=HIGHEST, preferred_element_type=jnp.float32)


def pack(ref, parts):
    at = 0
    row = lax.broadcasted_iota(jnp.int32, (TAIL, ref.shape[1]), 0)
    powers = jnp.zeros(row.shape, jnp.float32)
    for i, part in enumerate(parts):
        most = jnp.max(jnp.abs(part), axis=(0, 1), keepdims=True)
        power = jnp.floor(jnp.log2(jnp.maximum(most, 1e-30)))
        ref[at : at + part.shape[0], :] = part * jnp.exp2(14.0 - power)
        powers = jnp.where(row == i, power, powers)
        at += part.shape[0]
    ref[at:, :] = powers


def unpack(ref, at, length, i):
    row = ref.shape[0] - TAIL + i
    return ref[at : at + length, :] * jnp.exp2(ref[row : row + 1, :] - 14.0)


def in_hbm(value):
    return pltpu.with_memory_space_constraint(value, pltpu.HBM)


def upward_body(*refs):
    sources, targets, refs = refs[:6], refs[6:12], refs[12:]
    vec_ref, basis_ref, transfer_ref, cluster_ref, _, _ = targets
    first_ref, second_ref, coefs_ref, long_ref, short_ref, own_ref, sems = refs
    leaves, rank, rows = basis_ref.shape
    columns = vec_ref.shape[1]
    pairs = list(zip(sources, targets))
    pairs.append((sources[0].at[vec_ref.shape[0] - first_ref.shape[0] :, :], first_ref))
    pairs.append((sources[0].at[: second_ref.shape[0], :], second_ref))
    copies = [pltpu.make_async_copy(source, target, sems.at[i]) for i, (source, target) in enumerate(pairs)]
    for copy in copies:
        copy.start()
    for copy in copies[:4]:
        copy.wait()
    for leaf in range(leaves):
        coefs_ref[leaf * rank : (leaf + 1) * rank, :] = jnp.dot(
            basis_ref[leaf], vec_ref[leaf * rows : (leaf + 1) * rows, :], preferred_element_type=jnp.float32
        )
    whole = coefs_ref[...]
    transfer = transfer_ref[...].reshape(leaves * rank, rank)
    low = exact(transfer, whole, (0, 0))
    own_ref[...] = low
    matrix = cluster_ref[0]
    height = rank * rank // columns
    wide = jnp.concatenate([matrix[i : i + height, :] for i in range(0, rank, height)], axis=1)
    pack(long_ref, (whole, low, wide))
    short_ref[...] = long_ref[leaves * rank :, :]
    for copy in copies[4:]:
        copy.wait()


def upward(vectors, basis, transfer, cluster_transfer, cluster_coupling, top_coupling):
    leaves, rank, _ = basis.shape
    points, columns = vectors.shape
    f32 = jnp.float32
    arrays = (vectors, basis, transfer, cluster_transfer, cluster_coupling, top_coupling)
    short = rank + rank * rank // columns + TAIL
    return call(
        upward_body,
        [HBM] * 6,
        [(array.shape, array.dtype) for array in arrays]
        + [
            ((points // 2 + SPARE, columns), vectors.dtype),
            ((points // 2, columns), vectors.dtype),
            ((leaves * rank, columns), f32),
            ((leaves * rank + short, columns), f32),
            ((short, columns), f32),
            ((rank, columns), f32),
        ],
        scratch=[pltpu.SemaphoreType.DMA((8,))],
        name="leaf_and_cluster_coefs",
    )(*[in_hbm(array) for array in arrays])


def cluster_body(subs, own_ref, matrix_ref, low_ref, high_ref, *refs):
    part_refs, (stack_ref, top_ref) = refs[:-2], refs[-2:]
    rank = own_ref.shape[0]
    sub = lax.axis_index("sub")
    matrices, lows = [matrix_ref[0]], [own_ref[...]]

    columns = own_ref.shape[1]
    height = rank * rank // columns

    def put(valid, place, ref):
        at = ref.shape[0] - rank - height - TAIL
        low = unpack(ref, at, rank, 1)
        wide = unpack(ref, at + rank, height, 2)
        matrix = jnp.concatenate([wide[:, i : i + rank] for i in range(0, columns, rank)], axis=0)

        @pl.when(valid)
        def _():
            stack_ref[place] = low

        matrices.append(matrix)
        lows.append(jnp.where(valid, low, 0.0))

    stack_ref[sub] = own_ref[...]
    put(sub > 0, sub - 1, low_ref)
    put(sub < subs - 1, sub + 1, high_ref)
    for i, ref in enumerate(part_refs[:-1]):
        put(sub >= 0, lax.rem(sub - 2 - i + subs, subs), ref)
    if part_refs:
        put((sub == 0) | (sub == subs - 1), subs - 1 - sub, part_refs[-1])
    top_ref[0] = exact(jnp.concatenate(matrices, axis=0), jnp.concatenate(lows, axis=0), (0, 0))


def cluster_sums(own, matrix, low, high, parts):
    rank, columns = own.shape
    subs = lax.axis_size("sub")
    return call(
        functools.partial(cluster_body, subs),
        [VMEM] * (4 + len(parts)),
        [((subs, rank, columns), jnp.float32), ((1, rank, columns), jnp.float32)],
        name="sums_over_sub",
    )(own, matrix, low, high, *parts)


def join_body(first_ref, second_ref, out_ref):
    width = first_ref.shape[0]
    out_ref[:width] = first_ref[...]
    out_ref[width:] = second_ref[...]


def join(first, second):
    shape = (2 * first.shape[0],) + first.shape[1:]
    return call(join_body, [VMEM] * 2, [(shape, first.dtype)], name="join_cols")(first, second)[0]


def gather_sub(value):
    count = lax.axis_size("sub")
    return [
        lax.ppermute(value, "sub", [(i, (i + step) % count) for i in range(count)])
        for step in range(2, count - 1)
    ]


def onward_body(low_ref, high_ref, out_ref):
    at = low_ref.shape[0] - out_ref.shape[0]
    out_ref[...] = jnp.where(lax.axis_index("sub") == 0, low_ref[at:, :], high_ref[at:, :])


def around(low, high, length):
    subs, cols = lax.axis_size("sub"), lax.axis_size("col")
    onward = call(
        onward_body, [VMEM] * 2, [((length, low.shape[1]), jnp.float32)], name="passed_on"
    )(low, high)[0]
    pairs = []
    for col in range(cols):
        pairs.append((col * subs, (col - 1) % cols * subs))
        pairs.append((col * subs + subs - 1, (col + 1) % cols * subs + subs - 1))
    return lax.ppermute(onward.astype(jnp.float16), BOTH, pairs)


def gather_col(value):
    count = lax.axis_size("col")
    if count & (count - 1):
        return lax.all_gather(value, "col", axis=0, tiled=True)
    width = 1
    while width < count:
        pairs = [(i, i ^ width) for i in range(count)]
        value = join(value, lax.ppermute(value, "col", pairs))
        width *= 2
    return value


def split(value):
    head = value.astype(jnp.bfloat16)
    return head, (value - head.astype(jnp.float32)).astype(jnp.bfloat16)


def far_body(far_ref, near_ref, coupling_in, low_ref, own_ref, high_ref, field_ref, coupling_ref, heads, rests, sems):
    leaves, slots, rank, _ = coupling_ref.shape
    rows = leaves * rank

    def copy(leaf):
        return pltpu.make_async_copy(coupling_in.at[leaf], coupling_ref.at[leaf], sems.at[leaf])

    @pl.loop(0, leaves)
    def _(leaf):
        copy(leaf).start()

    first = near_ref[0, 0] - leaves
    for place, ref in ((0, low_ref), (2, high_ref)):
        here = slice(place * rows, (place + 1) * rows)
        heads[here, :], rests[here, :] = split(unpack(ref, 0, rows, 0))
    heads[rows : 2 * rows, :], rests[rows : 2 * rows, :] = split(own_ref[...])

    for leaf in range(leaves):
        copy(leaf).wait()
    for leaf in range(leaves):
        picked = []
        for k in range(slots):
            place = jnp.clip(far_ref[k, leaf] - first, 0, 3 * leaves - 1)
            picked.append(pl.ds(pl.multiple_of(place * rank, rank), rank))
        head = jnp.concatenate([heads[at, :] for at in picked], axis=0)
        rest = jnp.concatenate([rests[at, :] for at in picked], axis=0)
        here = coupling_ref[leaf]
        wide_head, wide_rest = split(jnp.concatenate([here[k] for k in range(slots)], axis=1))
        both = jnp.dot(
            jnp.concatenate([wide_head, wide_rest], axis=0), head, preferred_element_type=jnp.float32
        )
        last = jnp.dot(wide_head, rest, preferred_element_type=jnp.float32)
        field_ref[leaf * rank : (leaf + 1) * rank, :] = both[:rank] + (both[rank:] + last)


def far(leaf_far, near_index, coupling, low, own, high):
    leaves, _, rank, _ = coupling.shape
    return call(
        far_body,
        [SMEM] * 2 + [HBM] + [VMEM] * 3,
        [(own.shape, jnp.float32)],
        scratch=[
            pltpu.VMEM(coupling.shape, coupling.dtype),
            pltpu.VMEM((3 * leaves * rank, own.shape[1]), jnp.bfloat16),
            pltpu.VMEM((3 * leaves * rank, own.shape[1]), jnp.bfloat16),
            pltpu.SemaphoreType.DMA((leaves,)),
        ],
        name="far_field_of_leaves",
    )(leaf_far, near_index, in_hbm(coupling), low, own, high)[0]


def load_body(blocks_ref, held_ref, sem):
    copy = pltpu.make_async_copy(blocks_ref, held_ref, sem)
    copy.start()
    copy.wait()


def load(blocks):
    return pl.pallas_call(
        load_body,
        in_specs=[HBM],
        out_specs=VMEM,
        out_shape=pltpu.VMEM(blocks.shape, blocks.dtype),
        scratch_shapes=[pltpu.SemaphoreType.DMA],
        cost_estimate=pl.CostEstimate(flops=0, bytes_accessed=0, transcendentals=0),
        compiler_params=pltpu.CompilerParams(vmem_limit_bytes=16 * 2**20),
        name="load_near_blocks",
    )(in_hbm(blocks))


def near_body(
    near_ref, blocks_ref, own_ref, high_ref, acc_ref, list_ref, found_ref, window
):
    leaves, slots, rows, _ = blocks_ref.shape

    window[: leaves * rows, :] = own_ref[...]
    window[leaves * rows : 2 * leaves * rows, :] = high_ref[...]
    window[2 * leaves * rows :, :] = jnp.zeros((rows, high_ref.shape[1]), window.dtype)
    first = near_ref[0, 0]

    half = leaves // 2
    room = list_ref.shape[0] // 2
    lane = lax.broadcasted_iota(jnp.int32, (1, list_ref.shape[1]), 1)
    list_ref[...] = jnp.zeros_like(list_ref)

    def note(leaf, carry):
        mask, counts = carry
        for k in range(1, slots):
            place = near_ref[k, leaf] - first + leaves
            after = []
            for i, valid in enumerate((place >= half, place < half)):
                valid = valid & (place < leaves)
                at = jnp.maximum(place - (1 - i) * half, 0)
                entry = jnp.where(lane == 0, leaf * slots + k, jnp.where(lane == 1, at, 0))

                @pl.when(valid)
                def _(entry=entry, spot=i * room + counts[i]):
                    list_ref[pl.ds(spot, 1), :] = entry

                one = valid.astype(jnp.int32)
                after.append(counts[i] + one)
            counts = tuple(after)
            mask = mask | jnp.where(place < half, lax.shift_left(jnp.int32(1), leaf), 0)
        return mask, counts

    zero = jnp.int32(0)
    mask, counts = lax.fori_loop(0, leaves, note, (zero, (zero, zero)))
    found_ref[0:1, :] = jnp.broadcast_to(mask, lane.shape)
    found_ref[1:2, :] = jnp.where(lane == 0, counts[0], counts[1])

    for leaf in range(leaves):
        acc = None
        for k in range(slots):
            place = near_ref[k, leaf] - first
            place = jnp.where(place < 0, 2 * leaves, jnp.minimum(place, 2 * leaves - 1))
            start = pl.multiple_of(place * rows, rows)
            term = jnp.dot(
                blocks_ref[leaf, k], window[pl.ds(start, rows), :], preferred_element_type=jnp.float32
            )
            acc = term if acc is None else acc + term
        acc_ref[leaf * rows : (leaf + 1) * rows, :] = acc


def near(near_index, blocks, own, high):
    leaves, slots, rows, _ = blocks.shape
    room = leaves * slots + 2 * BATCH
    lanes = -(-max(leaves, 2) // 128) * 128
    return pl.pallas_call(
        near_body,
        in_specs=[SMEM] + [VMEM] * 3,
        out_specs=[VMEM] * 3,
        out_shape=[
            pltpu.VMEM(own.shape, jnp.float32),
            jax.ShapeDtypeStruct((2 * room, lanes), jnp.int32),
            jax.ShapeDtypeStruct((8, lanes), jnp.int32),
        ],
        scratch_shapes=[
            pltpu.VMEM(((2 * leaves + 1) * rows, own.shape[1]), own.dtype),
        ],
        compiler_params=pltpu.CompilerParams(vmem_limit_bytes=32 * 2**20),
        cost_estimate=pl.CostEstimate(flops=0, bytes_accessed=0, transcendentals=0),
        name="near_own_and_high",
    )(near_index, blocks, own, high)


def down_body(
    straight, partner_ref, top_partner_ref, stack_ref, cols_ref, coupling_ref, top_coupling_ref, cluster_ref,
    transfer_ref, field_ref, basis_ref, acc_ref, sum_ref, fields,
):
    leaves, rank, rows = basis_ref.shape
    col = lax.axis_index("col")
    slots = top_coupling_ref.shape[1]
    picked = []
    for k in range(slots):
        place = top_partner_ref[0, k]
        picked.append(cols_ref[place if straight else lax.bitwise_xor(place, col)])
    wide = jnp.concatenate([top_coupling_ref[0, k] for k in range(slots)], axis=1)
    top = exact(wide, jnp.concatenate(picked, axis=0))
    slots = coupling_ref.shape[1]
    picked = [stack_ref[partner_ref[0, k]] for k in range(slots)] + [top]
    wide = jnp.concatenate([coupling_ref[0, k] for k in range(slots)] + [cluster_ref[0]], axis=1)
    cluster = exact(wide, jnp.concatenate(picked, axis=0))
    transfer = transfer_ref[...].reshape(leaves * rank, rank)
    fields[...] = (field_ref[...] + exact(transfer, cluster)).astype(fields.dtype)
    for leaf in range(leaves):
        here = slice(leaf * rows, (leaf + 1) * rows)
        sum_ref[here, :] = acc_ref[here, :] + lax.dot_general(
            basis_ref[leaf],
            fields[leaf * rank : (leaf + 1) * rank, :],
            (((0,), (0,)), ((), ())),
            preferred_element_type=jnp.float32,
        )


def down(partner, top_partner, stack, cols, coupling, top_coupling, cluster_transfer, transfer, field, basis, acc):
    count = lax.axis_size("col")
    return pl.pallas_call(
        functools.partial(down_body, bool(count & (count - 1))),
        in_specs=[SMEM] * 2 + [VMEM] * 9,
        out_specs=VMEM,
        out_shape=pltpu.VMEM(acc.shape, jnp.float32),
        scratch_shapes=[pltpu.VMEM(field.shape, jnp.bfloat16)],
        compiler_params=pltpu.CompilerParams(vmem_limit_bytes=16 * 2**20),
        cost_estimate=pl.CostEstimate(flops=0, bytes_accessed=0, transcendentals=0),
        name="fields_down",
    )(partner, top_partner, stack, cols, coupling, top_coupling, cluster_transfer, transfer, field, basis, acc)


def add_listed(list_ref, found_ref, part, batch_size, blocks_ref, low_ref, acc_ref):
    _, slots, rows, _ = blocks_ref.shape
    count = found_ref[1, part]
    room = list_ref.shape[0] // 2

    def read(batch):
        spots = [part * room + batch * batch_size + i for i in range(batch_size)]
        return [(list_ref[spot, 0], list_ref[spot, 1]) for spot in spots]

    def add(batch, entries):
        coming = read(batch + 1)
        terms = []
        for at, place in entries:
            start = pl.multiple_of(place * rows, rows)
            block = blocks_ref[at // slots, lax.rem(at, slots)]
            terms.append(jnp.dot(block, low_ref[pl.ds(start, rows), :], preferred_element_type=jnp.float32))
        for i, (at, _) in enumerate(entries):
            start = pl.multiple_of(at // slots * rows, rows)
            term = jnp.where(batch * batch_size + i < count, terms[i], 0.0)
            acc_ref[pl.ds(start, rows), :] += term
        return coming

    lax.fori_loop(0, pl.cdiv(count, batch_size), add, read(0))


def write(leaves, chosen, acc_ref, out_ref, held, sems):
    rows = acc_ref.shape[0] // leaves

    def copy(leaf):
        here = slice(leaf * rows, (leaf + 1) * rows)
        return pltpu.make_async_copy(held.at[here, :], out_ref.at[here, :], sems.at[leaf])

    for leaf in range(leaves):

        @pl.when(chosen[leaf])
        def _(leaf=leaf):
            here = slice(leaf * rows, (leaf + 1) * rows)
            held[here, :] = acc_ref[here, :].astype(held.dtype)
            copy(leaf).start()

    for leaf in range(leaves):

        @pl.when(chosen[leaf])
        def _(leaf=leaf):
            copy(leaf).wait()


def first_body(list_ref, found_ref, blocks_ref, low_ref, acc_in, acc_ref, out_ref, held, sems):
    leaves = blocks_ref.shape[0]
    mask = found_ref[0, 0]
    final = [mask & (1 << leaf) == 0 for leaf in range(leaves)]
    add_listed(list_ref, found_ref, 0, BATCH, blocks_ref, low_ref.at[SPARE:, :], acc_ref)
    write(leaves, final, acc_ref, out_ref, held, sems)


def near_low(places, found, blocks, low, acc):
    leaves = blocks.shape[0]
    return pl.pallas_call(
        first_body,
        in_specs=[VMEM] * 5,
        out_specs=[VMEM, HBM],
        out_shape=[pltpu.VMEM(acc.shape, acc.dtype), pltpu.HBM(acc.shape, low.dtype)],
        input_output_aliases={4: 0},
        scratch_shapes=[
            pltpu.VMEM(acc.shape, low.dtype),
            pltpu.SemaphoreType.DMA((leaves,)),
        ],
        compiler_params=pltpu.CompilerParams(vmem_limit_bytes=16 * 2**20),
        cost_estimate=pl.CostEstimate(flops=0, bytes_accessed=0, transcendentals=0),
        name="near_low_first",
    )(places, found, blocks, low, acc)


def last_body(list_ref, found_ref, blocks_ref, low_ref, acc_ref, out_in, out_ref, held, sems):
    leaves = blocks_ref.shape[0]
    mask = found_ref[0, 0]
    touched = [mask & (1 << leaf) != 0 for leaf in range(leaves)]
    add_listed(list_ref, found_ref, 1, GROUP, blocks_ref, low_ref, acc_ref)
    write(leaves, touched, acc_ref, out_ref, held, sems)


def last(places, found, blocks, low, acc, out):
    leaves = blocks.shape[0]
    return pl.pallas_call(
        last_body,
        in_specs=[VMEM] * 5 + [HBM],
        out_specs=HBM,
        out_shape=jax.ShapeDtypeStruct(out.shape, out.dtype),
        input_output_aliases={5: 0},
        scratch_shapes=[
            pltpu.VMEM(out.shape, out.dtype),
            pltpu.SemaphoreType.DMA((leaves,)),
        ],
        compiler_params=pltpu.CompilerParams(vmem_limit_bytes=16 * 2**20),
        cost_estimate=pl.CostEstimate(flops=0, bytes_accessed=0, transcendentals=0),
        name="near_low_second",
    )(places, found, blocks, low, acc, out)


def local(
    vectors,
    near_blocks,
    near_index,
    leaf_basis,
    leaf_transfer,
    leaf_coupling,
    leaf_far,
    cluster_transfer,
    cluster_coupling,
    cluster_partner,
    top_coupling,
    top_partner,
):
    high_vec = shift(vectors, -1)
    near_index, leaf_far = near_index.T, leaf_far.T

    own, basis, transfer, cluster, couple, top_couple, first, second, coefs, long, short, own_low = upward(
        vectors, leaf_basis, leaf_transfer, cluster_transfer, cluster_coupling, top_coupling
    )
    long, short = long.astype(jnp.float16), short.astype(jnp.float16)
    low_part = shift_around(long, 1)
    high_part = shift_around(long, -1)
    parts = gather_sub(short)
    first, near_blocks, _ = lax.optimization_barrier((first, near_blocks, long))
    blocks = load(near_blocks)
    low_first = shift(first, 1)
    acc, places, found = near(near_index, blocks, own, high_vec)

    second, parts, low_part, high_part, acc = lax.optimization_barrier((second, parts, low_part, high_part, acc))
    low_second = shift(second, 1)

    low_part, high_part = low_part.astype(jnp.float32), high_part.astype(jnp.float32)
    if lax.axis_size("sub") > 2:
        parts = parts + [around(low_part, high_part, short.shape[0])]
    parts = [part.astype(jnp.float32) for part in parts]
    stack, top = cluster_sums(own_low, cluster, low_part, high_part, parts)
    cols = gather_col(top)
    field = far(leaf_far, near_index, leaf_coupling, low_part, coefs, high_part)
    acc = down(
        cluster_partner, top_partner, stack, cols, couple, top_couple, cluster, transfer, field, basis, acc
    )
    acc, out = near_low(places, found, blocks, low_first, acc)
    return last(places, found, blocks, low_second, acc, out)


def solution(mesh):
    both = P(BOTH)
    in_specs = (both,) * 10 + (P("col"),) * 2
    return jax.shard_map(local, mesh=mesh, in_specs=in_specs, out_specs=both, check_vma=False)
```

```python
import functools

import jax
import jax.numpy as jnp
from jax import lax
from jax.experimental import pallas as pl
from jax.experimental.pallas import tpu as pltpu
from jax.sharding import PartitionSpec as P

HIGHEST = lax.Precision.HIGHEST
BOTH = ("col", "sub")
SPARE = 16
TAIL = 8
GROUP = 6
BATCH = 8
VMEM = pl.BlockSpec(memory_space=pltpu.VMEM)
SMEM = pl.BlockSpec(memory_space=pltpu.SMEM)
HBM = pl.BlockSpec(memory_space=pltpu.HBM)


def call(body, ins, outs, scratch=(), mib=16, name=None):
    return pl.pallas_call(
        body,
        in_specs=ins,
        out_specs=[VMEM] * len(outs),
        out_shape=[jax.ShapeDtypeStruct(shape, kind) for shape, kind in outs],
        scratch_shapes=scratch,
        compiler_params=pltpu.CompilerParams(vmem_limit_bytes=mib * 2**20),
        cost_estimate=pl.CostEstimate(flops=0, bytes_accessed=0, transcendentals=0),
        name=name,
    )


def shift(value, step):
    count = lax.axis_size(BOTH)
    pairs = [(i, i + step) for i in range(count) if 0 <= i + step < count]
    return lax.ppermute(value, BOTH, pairs)


def shift_around(value, by):
    count = lax.axis_size(BOTH)
    return lax.ppermute(value, BOTH, [(i, (i + by) % count) for i in range(count)])


def exact(a, b, contract=(1, 0)):
    dims = (((contract[0],), (contract[1],)), ((), ()))
    return lax.dot_general(a, b, dims, precision=HIGHEST, preferred_element_type=jnp.float32)


def pack(ref, parts):
    at = 0
    row = lax.broadcasted_iota(jnp.int32, (TAIL, ref.shape[1]), 0)
    powers = jnp.zeros(row.shape, jnp.float32)
    for i, part in enumerate(parts):
        most = jnp.max(jnp.abs(part), axis=(0, 1), keepdims=True)
        power = jnp.floor(jnp.log2(jnp.maximum(most, 1e-30)))
        ref[at : at + part.shape[0], :] = part * jnp.exp2(14.0 - power)
        powers = jnp.where(row == i, power, powers)
        at += part.shape[0]
    ref[at:, :] = powers


def unpack(ref, at, length, i):
    row = ref.shape[0] - TAIL + i
    return ref[at : at + length, :] * jnp.exp2(ref[row : row + 1, :] - 14.0)


def in_hbm(value):
    return pltpu.with_memory_space_constraint(value, pltpu.HBM)


def upward_body(*refs):
    sources, targets, refs = refs[:6], refs[6:12], refs[12:]
    vec_ref, basis_ref, transfer_ref, cluster_ref, _, _ = targets
    first_ref, second_ref, coefs_ref, long_ref, short_ref, own_ref, sems = refs
    leaves, rank, rows = basis_ref.shape
    columns = vec_ref.shape[1]
    pairs = list(zip(sources, targets))
    pairs.append((sources[0].at[vec_ref.shape[0] - first_ref.shape[0] :, :], first_ref))
    pairs.append((sources[0].at[: second_ref.shape[0], :], second_ref))
    copies = [pltpu.make_async_copy(source, target, sems.at[i]) for i, (source, target) in enumerate(pairs)]
    for copy in copies:
        copy.start()
    for copy in copies[:4]:
        copy.wait()
    for leaf in range(leaves):
        coefs_ref[leaf * rank : (leaf + 1) * rank, :] = jnp.dot(
            basis_ref[leaf], vec_ref[leaf * rows : (leaf + 1) * rows, :], preferred_element_type=jnp.float32
        )
    whole = coefs_ref[...]
    transfer = transfer_ref[...].reshape(leaves * rank, rank)
    low = exact(transfer, whole, (0, 0))
    own_ref[...] = low
    matrix = cluster_ref[0]
    height = rank * rank // columns
    wide = jnp.concatenate([matrix[i : i + height, :] for i in range(0, rank, height)], axis=1)
    pack(long_ref, (whole, low, wide))
    short_ref[...] = long_ref[leaves * rank :, :]
    for copy in copies[4:]:
        copy.wait()


def upward(vectors, basis, transfer, cluster_transfer, cluster_coupling, top_coupling):
    leaves, rank, _ = basis.shape
    points, columns = vectors.shape
    f32 = jnp.float32
    arrays = (vectors, basis, transfer, cluster_transfer, cluster_coupling, top_coupling)
    short = rank + rank * rank // columns + TAIL
    return call(
        upward_body,
        [HBM] * 6,
        [(array.shape, array.dtype) for array in arrays]
        + [
            ((points // 2 + SPARE, columns), vectors.dtype),
            ((points // 2, columns), vectors.dtype),
            ((leaves * rank, columns), f32),
            ((leaves * rank + short, columns), f32),
            ((short, columns), f32),
            ((rank, columns), f32),
        ],
        scratch=[pltpu.SemaphoreType.DMA((8,))],
        name="leaf_and_cluster_coefs",
    )(*[in_hbm(array) for array in arrays])


def cluster_body(subs, own_ref, matrix_ref, low_ref, high_ref, *refs):
    part_refs, (stack_ref, top_ref) = refs[:-2], refs[-2:]
    rank = own_ref.shape[0]
    sub = lax.axis_index("sub")
    matrices, lows = [matrix_ref[0]], [own_ref[...]]

    columns = own_ref.shape[1]
    height = rank * rank // columns

    def put(valid, place, ref):
        at = ref.shape[0] - rank - height - TAIL
        low = unpack(ref, at, rank, 1)
        wide = unpack(ref, at + rank, height, 2)
        matrix = jnp.concatenate([wide[:, i : i + rank] for i in range(0, columns, rank)], axis=0)

        @pl.when(valid)
        def _():
            stack_ref[place] = low

        matrices.append(matrix)
        lows.append(jnp.where(valid, low, 0.0))

    stack_ref[sub] = own_ref[...]
    put(sub > 0, sub - 1, low_ref)
    put(sub < subs - 1, sub + 1, high_ref)
    for i, ref in enumerate(part_refs[:-1]):
        put(sub >= 0, lax.rem(sub - 2 - i + subs, subs), ref)
    if part_refs:
        put((sub == 0) | (sub == subs - 1), subs - 1 - sub, part_refs[-1])
    top_ref[0] = exact(jnp.concatenate(matrices, axis=0), jnp.concatenate(lows, axis=0), (0, 0))


def cluster_sums(own, matrix, low, high, parts):
    rank, columns = own.shape
    subs = lax.axis_size("sub")
    return call(
        functools.partial(cluster_body, subs),
        [VMEM] * (4 + len(parts)),
        [((subs, rank, columns), jnp.float32), ((1, rank, columns), jnp.float32)],
        name="sums_over_sub",
    )(own, matrix, low, high, *parts)


def join_body(first_ref, second_ref, out_ref):
    width = first_ref.shape[0]
    out_ref[:width] = first_ref[...]
    out_ref[width:] = second_ref[...]


def join(first, second):
    shape = (2 * first.shape[0],) + first.shape[1:]
    return call(join_body, [VMEM] * 2, [(shape, first.dtype)], name="join_cols")(first, second)[0]


def gather_sub(value):
    count = lax.axis_size("sub")
    return [
        lax.ppermute(value, "sub", [(i, (i + step) % count) for i in range(count)])
        for step in range(2, count - 1)
    ]


def onward_body(low_ref, high_ref, out_ref):
    at = low_ref.shape[0] - out_ref.shape[0]
    out_ref[...] = jnp.where(lax.axis_index("sub") == 0, low_ref[at:, :], high_ref[at:, :])


def around(low, high, length):
    subs, cols = lax.axis_size("sub"), lax.axis_size("col")
    onward = call(
        onward_body, [VMEM] * 2, [((length, low.shape[1]), jnp.float32)], name="passed_on"
    )(low, high)[0]
    pairs = []
    for col in range(cols):
        pairs.append((col * subs, (col - 1) % cols * subs))
        pairs.append((col * subs + subs - 1, (col + 1) % cols * subs + subs - 1))
    return lax.ppermute(onward.astype(jnp.float16), BOTH, pairs)


def gather_col(value):
    count = lax.axis_size("col")
    if count & (count - 1):
        return lax.all_gather(value, "col", axis=0, tiled=True)
    width = 1
    while width < count:
        pairs = [(i, i ^ width) for i in range(count)]
        value = join(value, lax.ppermute(value, "col", pairs))
        width *= 2
    return value


def split(value):
    head = value.astype(jnp.bfloat16)
    return head, (value - head.astype(jnp.float32)).astype(jnp.bfloat16)


def far_body(far_ref, near_ref, coupling_in, low_ref, own_ref, high_ref, field_ref, coupling_ref, heads, rests, sems):
    leaves, slots, rank, _ = coupling_ref.shape
    rows = leaves * rank

    def copy(leaf):
        return pltpu.make_async_copy(coupling_in.at[leaf], coupling_ref.at[leaf], sems.at[leaf])

    @pl.loop(0, leaves)
    def _(leaf):
        copy(leaf).start()

    first = near_ref[0, 0] - leaves
    for place, ref in ((0, low_ref), (2, high_ref)):
        here = slice(place * rows, (place + 1) * rows)
        heads[here, :], rests[here, :] = split(unpack(ref, 0, rows, 0))
    heads[rows : 2 * rows, :], rests[rows : 2 * rows, :] = split(own_ref[...])

    for leaf in range(leaves):
        copy(leaf).wait()
    for leaf in range(leaves):
        picked = []
        for k in range(slots):
            place = jnp.clip(far_ref[k, leaf] - first, 0, 3 * leaves - 1)
            picked.append(pl.ds(pl.multiple_of(place * rank, rank), rank))
        head = jnp.concatenate([heads[at, :] for at in picked], axis=0)
        rest = jnp.concatenate([rests[at, :] for at in picked], axis=0)
        here = coupling_ref[leaf]
        wide_head, wide_rest = split(jnp.concatenate([here[k] for k in range(slots)], axis=1))
        both = jnp.dot(
            jnp.concatenate([wide_head, wide_rest], axis=0), head, preferred_element_type=jnp.float32
        )
        last = jnp.dot(wide_head, rest, preferred_element_type=jnp.float32)
        field_ref[leaf * rank : (leaf + 1) * rank, :] = both[:rank] + (both[rank:] + last)


def far(leaf_far, near_index, coupling, low, own, high):
    leaves, _, rank, _ = coupling.shape
    return call(
        far_body,
        [SMEM] * 2 + [HBM] + [VMEM] * 3,
        [(own.shape, jnp.float32)],
        scratch=[
            pltpu.VMEM(coupling.shape, coupling.dtype),
            pltpu.VMEM((3 * leaves * rank, own.shape[1]), jnp.bfloat16),
            pltpu.VMEM((3 * leaves * rank, own.shape[1]), jnp.bfloat16),
            pltpu.SemaphoreType.DMA((leaves,)),
        ],
        name="far_field_of_leaves",
    )(leaf_far, near_index, in_hbm(coupling), low, own, high)[0]


def load_body(blocks_ref, held_ref, sem):
    copy = pltpu.make_async_copy(blocks_ref, held_ref, sem)
    copy.start()
    copy.wait()


def load(blocks):
    return pl.pallas_call(
        load_body,
        in_specs=[HBM],
        out_specs=VMEM,
        out_shape=pltpu.VMEM(blocks.shape, blocks.dtype),
        scratch_shapes=[pltpu.SemaphoreType.DMA],
        cost_estimate=pl.CostEstimate(flops=0, bytes_accessed=0, transcendentals=0),
        compiler_params=pltpu.CompilerParams(vmem_limit_bytes=16 * 2**20),
        name="load_near_blocks",
    )(in_hbm(blocks))


def near_body(
    near_ref, blocks_ref, own_ref, high_ref, acc_ref, list_ref, found_ref, window
):
    leaves, slots, rows, _ = blocks_ref.shape

    window[: leaves * rows, :] = own_ref[...]
    window[leaves * rows : 2 * leaves * rows, :] = high_ref[...]
    window[2 * leaves * rows :, :] = jnp.zeros((rows, high_ref.shape[1]), window.dtype)
    first = near_ref[0, 0]

    half = leaves // 2
    room = list_ref.shape[0] // 2
    lane = lax.broadcasted_iota(jnp.int32, (1, list_ref.shape[1]), 1)
    list_ref[...] = jnp.zeros_like(list_ref)

    def note(leaf, carry):
        mask, counts = carry
        for k in range(1, slots):
            place = near_ref[k, leaf] - first + leaves
            after = []
            for i, valid in enumerate((place >= half, place < half)):
                valid = valid & (place < leaves)
                at = jnp.maximum(place - (1 - i) * half, 0)
                entry = jnp.where(lane == 0, leaf * slots + k, jnp.where(lane == 1, at, 0))

                @pl.when(valid)
                def _(entry=entry, spot=i * room + counts[i]):
                    list_ref[pl.ds(spot, 1), :] = entry

                one = valid.astype(jnp.int32)
                after.append(counts[i] + one)
            counts = tuple(after)
            mask = mask | jnp.where(place < half, lax.shift_left(jnp.int32(1), leaf), 0)
        return mask, counts

    zero = jnp.int32(0)
    mask, counts = lax.fori_loop(0, leaves, note, (zero, (zero, zero)))
    found_ref[0:1, :] = jnp.broadcast_to(mask, lane.shape)
    found_ref[1:2, :] = jnp.where(lane == 0, counts[0], counts[1])

    for leaf in range(leaves):
        acc = None
        for k in range(slots):
            place = near_ref[k, leaf] - first
            place = jnp.where(place < 0, 2 * leaves, jnp.minimum(place, 2 * leaves - 1))
            start = pl.multiple_of(place * rows, rows)
            term = jnp.dot(
                blocks_ref[leaf, k], window[pl.ds(start, rows), :], preferred_element_type=jnp.float32
            )
            acc = term if acc is None else acc + term
        acc_ref[leaf * rows : (leaf + 1) * rows, :] = acc


def near(near_index, blocks, own, high):
    leaves, slots, rows, _ = blocks.shape
    room = leaves * slots + 2 * BATCH
    lanes = -(-max(leaves, 2) // 128) * 128
    return pl.pallas_call(
        near_body,
        in_specs=[SMEM] + [VMEM] * 3,
        out_specs=[VMEM] * 3,
        out_shape=[
            pltpu.VMEM(own.shape, jnp.float32),
            jax.ShapeDtypeStruct((2 * room, lanes), jnp.int32),
            jax.ShapeDtypeStruct((8, lanes), jnp.int32),
        ],
        scratch_shapes=[
            pltpu.VMEM(((2 * leaves + 1) * rows, own.shape[1]), own.dtype),
        ],
        compiler_params=pltpu.CompilerParams(vmem_limit_bytes=32 * 2**20),
        cost_estimate=pl.CostEstimate(flops=0, bytes_accessed=0, transcendentals=0),
        name="near_own_and_high",
    )(near_index, blocks, own, high)


def down_body(
    straight, partner_ref, top_partner_ref, stack_ref, cols_ref, coupling_ref, top_coupling_ref, cluster_ref,
    transfer_ref, field_ref, basis_ref, acc_ref, sum_ref, fields,
):
    leaves, rank, rows = basis_ref.shape
    col = lax.axis_index("col")
    slots = top_coupling_ref.shape[1]
    picked = []
    for k in range(slots):
        place = top_partner_ref[0, k]
        picked.append(cols_ref[place if straight else lax.bitwise_xor(place, col)])
    wide = jnp.concatenate([top_coupling_ref[0, k] for k in range(slots)], axis=1)
    top = exact(wide, jnp.concatenate(picked, axis=0))
    slots = coupling_ref.shape[1]
    picked = [stack_ref[partner_ref[0, k]] for k in range(slots)] + [top]
    wide = jnp.concatenate([coupling_ref[0, k] for k in range(slots)] + [cluster_ref[0]], axis=1)
    cluster = exact(wide, jnp.concatenate(picked, axis=0))
    transfer = transfer_ref[...].reshape(leaves * rank, rank)
    fields[...] = (field_ref[...] + exact(transfer, cluster)).astype(fields.dtype)
    for leaf in range(leaves):
        here = slice(leaf * rows, (leaf + 1) * rows)
        sum_ref[here, :] = acc_ref[here, :] + lax.dot_general(
            basis_ref[leaf],
            fields[leaf * rank : (leaf + 1) * rank, :],
            (((0,), (0,)), ((), ())),
            preferred_element_type=jnp.float32,
        )


def down(partner, top_partner, stack, cols, coupling, top_coupling, cluster_transfer, transfer, field, basis, acc):
    count = lax.axis_size("col")
    return pl.pallas_call(
        functools.partial(down_body, bool(count & (count - 1))),
        in_specs=[SMEM] * 2 + [VMEM] * 9,
        out_specs=VMEM,
        out_shape=pltpu.VMEM(acc.shape, jnp.float32),
        scratch_shapes=[pltpu.VMEM(field.shape, jnp.bfloat16)],
        compiler_params=pltpu.CompilerParams(vmem_limit_bytes=16 * 2**20),
        cost_estimate=pl.CostEstimate(flops=0, bytes_accessed=0, transcendentals=0),
        name="fields_down",
    )(partner, top_partner, stack, cols, coupling, top_coupling, cluster_transfer, transfer, field, basis, acc)


def add_listed(list_ref, found_ref, part, batch_size, blocks_ref, low_ref, acc_ref):
    _, slots, rows, _ = blocks_ref.shape
    count = found_ref[1, part]
    room = list_ref.shape[0] // 2

    def read(batch):
        spots = [part * room + batch * batch_size + i for i in range(batch_size)]
        return [(list_ref[spot, 0], list_ref[spot, 1]) for spot in spots]

    def add(batch, entries):
        coming = read(batch + 1)
        terms = []
        for at, place in entries:
            start = pl.multiple_of(place * rows, rows)
            block = blocks_ref[at // slots, lax.rem(at, slots)]
            terms.append(jnp.dot(block, low_ref[pl.ds(start, rows), :], preferred_element_type=jnp.float32))
        for i, (at, _) in enumerate(entries):
            start = pl.multiple_of(at // slots * rows, rows)
            term = jnp.where(batch * batch_size + i < count, terms[i], 0.0)
            acc_ref[pl.ds(start, rows), :] += term
        return coming

    lax.fori_loop(0, pl.cdiv(count, batch_size), add, read(0))


def write(leaves, chosen, acc_ref, out_ref, held, sems):
    rows = acc_ref.shape[0] // leaves

    def copy(leaf):
        here = slice(leaf * rows, (leaf + 1) * rows)
        return pltpu.make_async_copy(held.at[here, :], out_ref.at[here, :], sems.at[leaf])

    for leaf in range(leaves):

        @pl.when(chosen[leaf])
        def _(leaf=leaf):
            here = slice(leaf * rows, (leaf + 1) * rows)
            held[here, :] = acc_ref[here, :].astype(held.dtype)
            copy(leaf).start()

    for leaf in range(leaves):

        @pl.when(chosen[leaf])
        def _(leaf=leaf):
            copy(leaf).wait()


def first_body(list_ref, found_ref, blocks_ref, low_ref, acc_in, acc_ref, out_ref, held, sems):
    leaves = blocks_ref.shape[0]
    mask = found_ref[0, 0]
    final = [mask & (1 << leaf) == 0 for leaf in range(leaves)]
    add_listed(list_ref, found_ref, 0, BATCH, blocks_ref, low_ref.at[SPARE:, :], acc_ref)
    write(leaves, final, acc_ref, out_ref, held, sems)


def near_low(places, found, blocks, low, acc):
    leaves = blocks.shape[0]
    return pl.pallas_call(
        first_body,
        in_specs=[VMEM] * 5,
        out_specs=[VMEM, HBM],
        out_shape=[pltpu.VMEM(acc.shape, acc.dtype), pltpu.HBM(acc.shape, low.dtype)],
        input_output_aliases={4: 0},
        scratch_shapes=[
            pltpu.VMEM(acc.shape, low.dtype),
            pltpu.SemaphoreType.DMA((leaves,)),
        ],
        compiler_params=pltpu.CompilerParams(vmem_limit_bytes=16 * 2**20),
        cost_estimate=pl.CostEstimate(flops=0, bytes_accessed=0, transcendentals=0),
        name="near_low_first",
    )(places, found, blocks, low, acc)


def last_body(list_ref, found_ref, blocks_ref, low_ref, acc_ref, out_in, out_ref, held, sems):
    leaves = blocks_ref.shape[0]
    mask = found_ref[0, 0]
    touched = [mask & (1 << leaf) != 0 for leaf in range(leaves)]
    add_listed(list_ref, found_ref, 1, GROUP, blocks_ref, low_ref, acc_ref)
    write(leaves, touched, acc_ref, out_ref, held, sems)


def last(places, found, blocks, low, acc, out):
    leaves = blocks.shape[0]
    return pl.pallas_call(
        last_body,
        in_specs=[VMEM] * 5 + [HBM],
        out_specs=HBM,
        out_shape=jax.ShapeDtypeStruct(out.shape, out.dtype),
        input_output_aliases={5: 0},
        scratch_shapes=[
            pltpu.VMEM(out.shape, out.dtype),
            pltpu.SemaphoreType.DMA((leaves,)),
        ],
        compiler_params=pltpu.CompilerParams(vmem_limit_bytes=16 * 2**20),
        cost_estimate=pl.CostEstimate(flops=0, bytes_accessed=0, transcendentals=0),
        name="near_low_second",
    )(places, found, blocks, low, acc, out)


def local(
    vectors,
    near_blocks,
    near_index,
    leaf_basis,
    leaf_transfer,
    leaf_coupling,
    leaf_far,
    cluster_transfer,
    cluster_coupling,
    cluster_partner,
    top_coupling,
    top_partner,
):
    high_vec = shift(vectors, -1)
    near_index, leaf_far = near_index.T, leaf_far.T

    own, basis, transfer, cluster, couple, top_couple, first, second, coefs, long, short, own_low = upward(
        vectors, leaf_basis, leaf_transfer, cluster_transfer, cluster_coupling, top_coupling
    )
    long, short = long.astype(jnp.float16), short.astype(jnp.float16)
    low_part = shift_around(long, 1)
    high_part = shift_around(long, -1)
    parts = gather_sub(short)
    first, near_blocks, _ = lax.optimization_barrier((first, near_blocks, long))
    blocks = load(near_blocks)
    low_first = shift(first, 1)
    acc, places, found = near(near_index, blocks, own, high_vec)

    second, parts, low_part, high_part, acc = lax.optimization_barrier((second, parts, low_part, high_part, acc))
    low_second = shift(second, 1)

    low_part, high_part = low_part.astype(jnp.float32), high_part.astype(jnp.float32)
    if lax.axis_size("sub") > 2:
        parts = parts + [around(low_part, high_part, short.shape[0])]
    parts = [part.astype(jnp.float32) for part in parts]
    stack, top = cluster_sums(own_low, cluster, low_part, high_part, parts)
    cols = gather_col(top)
    field = far(leaf_far, near_index, leaf_coupling, low_part, coefs, high_part)
    acc = down(
        cluster_partner, top_partner, stack, cols, couple, top_couple, cluster, transfer, field, basis, acc
    )
    acc, out = near_low(places, found, blocks, low_first, acc)
    return last(places, found, blocks, low_second, acc, out)


def solution(mesh):
    both = P(BOTH)
    in_specs = (both,) * 10 + (P("col"),) * 2
    return jax.shard_map(local, mesh=mesh, in_specs=in_specs, out_specs=both, check_vma=False)
```
